32 devices in a mesh: group: 2 (over y), expert: 4 (over z), dp: 4 (over x, core).
Axes of the slice: x: 2, y: 2, z: 4, core: 2. Of those that a mesh axis runs over, the one named last changes fastest.
Arguments:
- tokens: bfloat16 [128, 4096], P(('group', 'expert', 'dp')), parts along dimension 0, may hold values from -6 to 6
- expert_ids: int32 [128, 8], P(('group', 'expert', 'dp')), parts along dimension 0, may hold values from 0 to 15, all different within a row; in each aligned block of 4 rows (0 to 3, 4 to 7, ...) at most 3 rows name the same one
- route_weight: float32 [128, 8], P(('group', 'expert', 'dp')), parts along dimension 0, may hold values from 0.1 to 1
- tenant_ids: int32 [128], P(('group', 'expert', 'dp')), parts along dimension 0, may hold values from 0 to 7
- gate_weight: bfloat16 [16, 4096, 1536], P('expert', None, 'dp'), may hold values from -0.09375 to 0.09375
- up_weight: bfloat16 [16, 4096, 1536], P('expert', None, 'dp'), may hold values from -0.09375 to 0.09375
- down_weight: bfloat16 [16, 1536, 4096], P('expert', None, 'dp'), may hold values from -0.15625 to 0.15625
- pool_shrink: bfloat16 [16, 8, 16, 1536], P('expert', 'dp'), may hold values from -0.15625 to 0.15625
- adapter_pool_expand: bfloat16 [16, 8, 16, 4096], P('expert', 'dp'), may hold values from -1.5 to 1.5
- page_owner: int32 [8, 16], replicated, may hold values from 0 to 3, as said below
- page_slot: int32 [8, 16], replicated, may hold values from 0 to 1, as said below
Outputs:
- mixed_out: bfloat16 [128, 4096], P(('group', 'expert', 'dp')), parts along dimension 0
The draws below stay inside these ranges and needn't reach their ends.
There are 2 independent parts, one for each index of `group`. The reference program is written for one: setup_inputs(seed, part) draws one part's arguments, and reference() takes and returns one part's arrays. A program takes and returns all parts, laid end to end along the dimension named above; an argument that names none is the same for every part. Nothing has to cross between parts.
Inputs may be any that keep to these rules, and one draw needn't show every extreme that they name: `expert_ids`: each row names 8 different experts; in the rows of one device no expert is named more than 3 times, a bound that some block reaches. For each expert, the pairs (page_owner, page_slot) of all tenants are all different. `page_slot`: see page_owner.
All inputs are finite; a program needn't handle non-finite values.
Results may differ from the reference program's by a relative error of at most 0.0062.
Values may be sent and summed in bfloat16 or wider, within the bound.
No kernel may reach another device: no remote copies, remote signals or barrier semaphores. Data moves between devices by JAX's collectives and lax.ppermute only.
A program may use at most 128 MiB of HBM per device.

```python
import math
import jax
import jax.numpy as jnp
import numpy as np
from jax import lax

MODEL_DIM = 4096
FF = 1536
TOP = 8
EXPERTS = 16
ADAPTER_RANK = 16
SLOTS = 2
TOK_DEV = 4
CAP = 3
TOKENS = 64
TENANT_COUNT = 8


def page_order(key):
    keys = jax.random.split(key, EXPERTS)
    orders = jax.vmap(lambda single: jax.random.permutation(single, TENANT_COUNT))(keys)
    return jnp.transpose(orders).astype(jnp.int32)


def draw_page_owner(key, part):
    placed = page_order(key)
    return placed // SLOTS


def draw_page_slot(key, part):
    placed = page_order(key)
    return placed % SLOTS


def place_ends(entries, stream_key, smallest, top_value):
    dims = entries.shape
    index_at = [jax.random.randint(jax.random.fold_in(stream_key, axis), (), 0, dims[axis]) for axis in range(len(dims))]
    entries = entries.at[tuple(index_at)].set(smallest)
    longest = dims.index(max(dims))
    index_at[longest] = (index_at[longest] + 1) % dims[longest]
    return entries.at[tuple(index_at)].set(top_value)


def steps_of(own_key, dims, cuts, least, largest):
    loudness = 1.0
    for position, shards_of in cuts:
        heights = jax.random.uniform(jax.random.fold_in(jax.random.fold_in(own_key, 6), position), (shards_of,), jnp.float32, least / len(cuts), largest / len(cuts))
        loudness = loudness * jnp.repeat(jnp.exp(heights), dims[position] // shards_of).reshape((-1,) + (1,) * (len(dims) - 1 - position))
    return loudness


def assign_block(key, own, number, rows, number_of, top, limit, slope):
    ranking = jax.random.permutation(key, number_of)
    heavy_load, usual = portions_of(number_of, rows * top, limit, slope, True), portions_of(number_of, rows * top, limit, slope, False)
    places = jnp.arange(number_of)

    def named(sizes, offset_by):
        used = int((sizes > 0).sum())
        fixed = max(1, used // 4)
        passed = fixed + (places - fixed + offset_by * (used - fixed)) % max(1, number_of - fixed)
        return jnp.zeros((number_of,), jnp.int32).at[ranking[jnp.where(places < fixed, places, passed)]].set(jnp.asarray(sizes, jnp.int32))

    sizes = jnp.where(number % 4 == 0, named(heavy_load, number // 4), named(usual, number - number // 4 - 1))
    mixed = jax.random.permutation(jax.random.fold_in(own, 3), number_of)
    giver, sink = mixed[0:number_of // 2 * 2:2], mixed[1:number_of // 2 * 2:2]
    room = jnp.minimum(sizes[giver] - 1, limit - sizes[sink]) // 2
    room = jnp.where((giver == ranking[0]) | (sink == ranking[0]) | (sizes[sink] == 0), 0, jnp.maximum(room, 0))
    passed = jax.random.randint(jax.random.fold_in(own, 4), (number_of // 2,), 0, 1 << 20) % (room + 1)
    sizes = sizes.at[giver].add(-passed).at[sink].add(passed)
    members = jnp.searchsorted(jnp.cumsum(sizes), jnp.arange(rows * top), side="right").astype(jnp.int32)
    listing = members.reshape(top, rows).T
    listing = listing[jax.random.permutation(jax.random.fold_in(own, 1), rows)]
    offset_by = jax.random.randint(jax.random.fold_in(own, 2), (rows, 1), 0, top)
    return jnp.take_along_axis(listing, (jnp.arange(top)[None, :] + offset_by) % top, axis=1)


def portions_of(count, total, bound, skew, full):
    portions = [(1 << 20) // math.isqrt(grade ** skew) + 1 for grade in range(1, count + 1)]
    largest = bound if full else min(bound, max(-(-total // count), total * portions[0] // sum(portions)))
    least = 1 if total - largest >= count - 1 else 0
    given, surplus = [largest] + [least] * (count - 1), total - largest - least * (count - 1)
    while surplus > 0:
        candidates = [i for i in range(1, count) if given[i] < largest] or [i for i in range(1, count) if given[i] < bound]
        pool, remaining = sum([portions[i] for i in candidates]), surplus
        for i in candidates:
            more = min(bound - given[i], max(1, remaining * portions[i] // pool), surplus)
            given[i] = given[i] + more
            surplus = surplus - more
    return np.array(given)


def noise(rng, dims, deviation, limit, pieces=(), kind=jnp.bfloat16):
    array = deviation * jax.random.normal(rng, dims, jnp.float32)
    if pieces:
        array = array * steps_of(rng, dims, pieces, -0.22, 0.18)
    return jnp.clip(array, -limit, limit).astype(kind)


def setup_inputs(seed: int = 0, part: int = 0) -> dict:
    seeds = jax.random.split(jax.random.key(seed), 12)
    part_keys = jax.random.split(jax.random.fold_in(seeds[11], part), 12)
    tokens = noise(part_keys[0], (TOKENS, MODEL_DIM), 1.0, 6.0, ((0, 16),))
    expert_ids_keys = jax.random.split(jax.random.fold_in(part_keys[1], 1), TOKENS // TOK_DEV)
    expert_ids_turns = jax.random.permutation(jax.random.fold_in(part_keys[1], 3), TOKENS // TOK_DEV)
    expert_ids = jax.vmap(lambda own, number: assign_block(jax.random.fold_in(part_keys[1], 2), own, number, TOK_DEV, EXPERTS, TOP, CAP, 2))(expert_ids_keys, expert_ids_turns).reshape((TOKENS, TOP))
    route_weight = jnp.clip(0.1 + 0.9 * jax.random.uniform(part_keys[2], (TOKENS, TOP), jnp.float32) ** steps_of(part_keys[2], (TOKENS, TOP), ((0, 16),), -0.2, 0.2), 0.1, 1.0)
    tenant_ids = place_ends(jax.random.randint(part_keys[3], (TOKENS,), 0, TENANT_COUNT), jax.random.fold_in(part_keys[3], 1), 0, TENANT_COUNT - 1).astype(jnp.int32)
    gate_weight = noise(seeds[4], (EXPERTS, MODEL_DIM, FF), MODEL_DIM ** -0.5, 0.09375, ((0, 4), (2, 4)))
    up_weight = noise(seeds[5], (EXPERTS, MODEL_DIM, FF), MODEL_DIM ** -0.5, 0.09375, ((0, 4), (2, 4)))
    down_weight = noise(seeds[6], (EXPERTS, FF, MODEL_DIM), FF ** -0.5, 0.15625, ((0, 4), (2, 4)))
    pool_shrink = noise(seeds[7], (EXPERTS, TENANT_COUNT, ADAPTER_RANK, FF), FF ** -0.5, 0.15625, ((0, 4), (1, 4)))
    adapter_pool_expand = noise(seeds[8], (EXPERTS, TENANT_COUNT, ADAPTER_RANK, MODEL_DIM), ADAPTER_RANK ** -0.5, 1.5, ((0, 4), (1, 4)))
    page_owner = draw_page_owner(jax.random.fold_in(seeds[11], 71), part)
    page_slot = draw_page_slot(jax.random.fold_in(seeds[11], 71), part)
    return {"tokens": tokens, "expert_ids": expert_ids, "route_weight": route_weight, "tenant_ids": tenant_ids, "gate_weight": gate_weight, "up_weight": up_weight, "down_weight": down_weight, "pool_shrink": pool_shrink, "adapter_pool_expand": adapter_pool_expand, "page_owner": page_owner, "page_slot": page_slot}


def reference(tokens, expert_ids, route_weight, tenant_ids, gate_weight, up_weight, down_weight, pool_shrink, adapter_pool_expand, page_owner, page_slot):
    row_bound = CAP * (TOKENS // TOK_DEV)
    global_slot = page_owner * SLOTS + page_slot

    def one_expert(running, expert_position):
        matched = expert_ids == expert_position
        weight = jnp.sum(jnp.where(matched, route_weight, 0.0), axis=1)
        routed = jnp.any(matched, axis=1)
        picked = jnp.nonzero(routed, size=row_bound, fill_value=0)[0].astype(jnp.int32)
        live_count = jnp.sum(routed.astype(jnp.int32))
        is_live = jnp.arange(row_bound, dtype=jnp.int32) < live_count
        token_rows = tokens[picked]
        gate_proj = jnp.dot(token_rows, gate_weight[expert_position], preferred_element_type=jnp.float32)
        up_proj = jnp.dot(token_rows, up_weight[expert_position], preferred_element_type=jnp.float32)
        hidden = (jax.nn.silu(gate_proj) * up_proj).astype(jnp.bfloat16)
        base_output = jnp.dot(hidden, down_weight[expert_position], preferred_element_type=jnp.float32)
        shrink_table = pool_shrink[expert_position].reshape(TENANT_COUNT * ADAPTER_RANK, FF)
        shrink = jnp.dot(hidden, shrink_table.T, preferred_element_type=jnp.float32).astype(jnp.bfloat16)
        slot_row = global_slot[tenant_ids[picked], expert_position].astype(jnp.int32)
        selector = (slot_row[:, None] == jnp.arange(TENANT_COUNT, dtype=jnp.int32)[None, :]).astype(jnp.bfloat16)
        masked_rows = (shrink.reshape(row_bound, TENANT_COUNT, ADAPTER_RANK) * selector[:, :, None]).reshape(row_bound, TENANT_COUNT * ADAPTER_RANK)
        adapter_update = jnp.dot(masked_rows, adapter_pool_expand[expert_position].reshape(TENANT_COUNT * ADAPTER_RANK, MODEL_DIM), preferred_element_type=jnp.float32)
        final_output = lax.optimization_barrier((base_output + adapter_update).astype(jnp.bfloat16)).astype(jnp.float32)
        scale = jnp.where(is_live, weight[picked], 0.0)
        running = running.at[picked].add(scale[:, None] * final_output)
        return running, None

    running, unused = lax.scan(one_expert, jnp.zeros((TOKENS, MODEL_DIM), jnp.float32), jnp.arange(EXPERTS, dtype=jnp.int32))
    return running.astype(jnp.bfloat16)
```

```python
import functools

import jax
import jax.numpy as jnp
from jax import lax
from jax.experimental import pallas as pl
from jax.experimental.pallas import tpu as pltpu
from jax.sharding import PartitionSpec as P

TOP = 8
EXPERTS = 16
SLOTS = 2
LANES = 128
BF = jnp.bfloat16
F32 = jnp.float32

VM = pl.BlockSpec(memory_space=pltpu.VMEM)
SM = pl.BlockSpec(memory_space=pltpu.SMEM)
HB = pl.BlockSpec(memory_space=pltpu.HBM)
ANY = pl.BlockSpec(memory_space=pl.ANY)


def in_vmem(x):
    return pltpu.with_memory_space_constraint(x, pltpu.VMEM)


def in_hbm(x):
    return pltpu.with_memory_space_constraint(x, pltpu.HBM)


def call(body, out_shape, operands, specs, limit, bytes_moved=0, scratch=()):
    return pl.pallas_call(
        body,
        out_shape=out_shape,
        in_specs=specs,
        out_specs=jax.tree.map(lambda _: VM, out_shape),
        scratch_shapes=scratch,
        cost_estimate=pl.CostEstimate(flops=0, bytes_accessed=bytes_moved, transcendentals=0),
        compiler_params=pltpu.CompilerParams(vmem_limit_bytes=limit),
    )(*operands)


def size_of(*arrays):
    total = 0
    for a in arrays:
        n = a.dtype.itemsize
        for s in a.shape[:-1]:
            n *= s
        total += n * (-(-a.shape[-1] // LANES) * LANES)
    return total


def prepare(*refs):
    y, held, sems = refs[6], refs[7:13], refs[13]
    copies = [pltpu.make_async_copy(refs[i], held[i], sems.at[i]) for i in range(6)]
    for c in copies:
        c.start()
    for c in copies:
        c.wait()
    ten, tok, ids, rw, owner, slot = held
    rows, width = tok.shape
    y[:, :width] = tok[...]
    lane = lax.broadcasted_iota(jnp.int32, (rows, LANES), 1)
    expert, piece = lane % EXPERTS, lane // EXPERTS
    w = jnp.zeros((rows, LANES), F32)
    for k in range(TOP):
        w += jnp.where(ids[:, k : k + 1] == expert, rw[:, k : k + 1], 0.0)
    high = w.astype(BF).astype(F32)
    mid = (w - high).astype(BF).astype(F32)
    low = w - high - mid
    y[:, width : width + LANES] = jnp.where(
        piece == 0, high, jnp.where(piece == 1, mid, jnp.where(piece == 2, low, 0.0))
    ).astype(BF)
    y[:, width + LANES :] = jnp.zeros((rows, LANES), BF)
    pages = [
        owner[pl.ds(ten[r], 1), :] * SLOTS + slot[pl.ds(ten[r], 1), :] for r in range(rows)
    ]
    y[:, width + LANES : width + LANES + EXPERTS] = (
        jnp.concatenate(pages, axis=0).astype(F32).astype(BF)
    )


def fetch(experts, dep, *refs):
    del dep
    count = len(experts)
    sems = refs[-1]
    copies = []
    for i, pick in enumerate(experts):
        src, dst = refs[i], refs[count + i]
        for j, e in enumerate(pick):
            copies.append(pltpu.make_async_copy(src.at[e], dst.at[j], sems.at[len(copies)]))
    for c in copies:
        c.start()
    for c in copies:
        c.wait()


def prefetch(dep, arrays, picks):
    shapes = [pltpu.VMEM((len(p),) + a.shape[1:], a.dtype) for a, p in zip(arrays, picks)]
    moved = sum(size_of(a) * len(p) // a.shape[0] for a, p in zip(arrays, picks))
    out = pl.pallas_call(
        functools.partial(fetch, picks),
        out_shape=shapes,
        in_specs=[ANY] + [HB] * len(arrays),
        out_specs=[VM] * len(arrays),
        scratch_shapes=[pltpu.SemaphoreType.DMA((sum(len(p) for p in picks),))],
        cost_estimate=pl.CostEstimate(flops=0, bytes_accessed=2 * moved, transcendentals=0),
        compiler_params=pltpu.CompilerParams(vmem_limit_bytes=1 << 20),
    )(dep, *[in_hbm(a) for a in arrays])
    return out


def join(count, *refs):
    out = refs[-1]
    out[...] = jnp.concatenate([r[...].astype(F32) for r in refs[:count]], axis=0).astype(BF)


def up_kernel(count, parts, *refs):
    x_refs, refs = refs[:count], refs[count:]
    held, refs = refs[: len(parts)], refs[len(parts) :]
    gate_hbm, up_hbm, h, slots, late, sems = refs
    experts, width = gate_hbm.shape[0], gate_hbm.shape[1]
    source = {"g": gate_hbm, "u": up_hbm}
    where_is, copies = {}, {}
    for ref, (kind, pick) in zip(held, parts):
        for j, e in enumerate(pick):
            where_is[kind, e] = (ref, j)
    spot = 0
    for e in range(experts):
        for kind in "gu":
            if (kind, e) not in where_is:
                copies[kind, e] = pltpu.make_async_copy(
                    source[kind].at[e], late.at[spot], sems.at[spot]
                )
                copies[kind, e].start()
                where_is[kind, e] = (late, spot)
                spot += 1
    first = lax.axis_index("expert") * experts
    x = jnp.concatenate([r[:, :width] for r in x_refs], axis=0)
    meta = jnp.concatenate([r[:, width : width + LANES] for r in x_refs], axis=0).astype(F32)
    slots[...] = jnp.concatenate([r[:, width + LANES :] for r in x_refs], axis=0)
    lane = lax.broadcasted_iota(jnp.int32, meta.shape, 1)

    def weights(kind, e):
        if (kind, e) in copies:
            copies[kind, e].wait()
        ref, j = where_is[kind, e]
        return ref[j]

    for e in range(experts):
        w = jnp.sum(jnp.where(lane % EXPERTS == first + e, meta, 0.0), axis=1, keepdims=True)
        a = jnp.dot(x, weights("g", e), preferred_element_type=F32)
        b = jnp.dot(x, weights("u", e), preferred_element_type=F32)
        h[e] = (a * jax.nn.sigmoid(a) * b * w).astype(BF)


def down_kernel(offs, block, *refs):
    n = len(offs)
    h_refs, refs = refs[:n], refs[n:]
    slots_ref, down, shrink, expand, keep, send, hs = refs
    me = lax.axis_index("dp")
    experts, rows, part = h_refs[0].shape
    first = lax.axis_index("expert") * experts
    for i, m in enumerate(offs):
        for p in range(n):
            q = offs.index(offs[p] ^ m)
            hs[me ^ m, :, p * block : (p + 1) * block, :] = h_refs[i][
                :, q * block : (q + 1) * block, :
            ]
    per = shrink.shape[0] // experts
    rank = per // SLOTS
    slot_values = slots_ref[...].astype(F32)
    lane16 = lax.broadcasted_iota(jnp.int32, slot_values.shape, 1)
    lane = lax.broadcasted_iota(jnp.int32, (rows, shrink.shape[0]), 1)
    wanted = me * SLOTS + (lane % per) // rank
    base = None
    small = jnp.zeros((rows, shrink.shape[0]), F32)
    joined = part % LANES == 0
    for e in range(experts):
        chosen = jnp.sum(
            jnp.where(lane16 == first + e, slot_values, 0.0), axis=1, keepdims=True
        ).astype(jnp.int32)
        pieces = [hs[c, e] for c in range(n)]
        cuts = [(c * part, (c + 1) * part) for c in range(n)]
        if joined:
            pieces, cuts = [jnp.concatenate(pieces, axis=1)], [(0, n * part)]
        full = jnp.zeros((rows, shrink.shape[0]), F32)
        for x, (lo, hi) in zip(pieces, cuts):
            term = jnp.dot(x, down[e, lo:hi, :], preferred_element_type=F32)
            base = term if base is None else base + term
            full += lax.dot_general(
                x, shrink[:, lo:hi], (((1,), (1,)), ((), ())), preferred_element_type=F32
            )
        small = jnp.where((lane // per == e) & (chosen == wanted), full, small)
    small = small.astype(BF)
    cols = base.shape[1]
    half = rows // 2
    for c in range(n):
        here = slice(c * cols, (c + 1) * cols)
        out = jnp.dot(small, expand[:, here], preferred_element_type=F32)
        out += jnp.where(me == c, base, 0.0)
        keep[:, here] = out[:half]
        send[:, here] = out[half:].astype(BF)


def halve(keep, got, new_keep, new_send):
    total = keep[...] + got[...].astype(F32)
    half = total.shape[0] // 2
    new_keep[...] = total[:half]
    new_send[...] = total[half:].astype(BF)


def split_rows(block, keep, got, own, *sends):
    total = keep[...] + got[...].astype(F32)
    own[...] = total[:block]
    for i, s in enumerate(sends):
        s[...] = total[(i + 1) * block : (i + 2) * block].astype(BF)


def finish(own, *refs):
    total = own[...]
    for r in refs[:-1]:
        total += r[...].astype(F32)
    refs[-1][...] = total.astype(BF)


def shards(tokens, expert_ids, route_weight, tenant_ids, gate, up, down, shrink, expand, owner, slot):
    n_z, n_dp = lax.axis_size("expert"), lax.axis_size("dp")
    rows, width = tokens.shape
    experts, _, part = gate.shape
    wide = width + 2 * LANES
    all_rows = rows * n_z * n_dp
    block = rows * n_z

    def over(x, axis, m):
        size = lax.axis_size(axis)
        return lax.ppermute(x, axis, [(i, i ^ m) for i in range(size)])

    roomy = 16 << 20
    inputs = (tenant_ids, tokens, expert_ids, route_weight, owner, slot)
    with jax.named_scope("prepare"):
        y = call(
            prepare,
            jax.ShapeDtypeStruct((rows, wide), BF),
            [in_hbm(a) for a in inputs],
            [HB] * len(inputs),
            roomy,
            scratch=[
                *[(pltpu.VMEM if i else pltpu.SMEM)(a.shape, a.dtype) for i, a in enumerate(inputs)],
                pltpu.SemaphoreType.DMA((len(inputs),)),
            ],
        )

    early = [[0], [1, 2], [1]] if experts >= 4 else [[], [], []]
    got = [over(y, "expert", k) for k in range(1, n_z)]
    held, parts = [], []
    if early[0]:
        g0, u0 = prefetch(y, [gate, up], [early[0], early[0]])
        held += [g0, u0]
        parts += [("g", early[0]), ("u", early[0])]
    blocks = [
        call(
            functools.partial(join, n_z),
            jax.ShapeDtypeStruct((block, wide), BF),
            (y, *got, *[in_vmem(a) for a in held]),
            [VM] * (n_z + len(held)),
            roomy,
        )
    ]
    offs = [0]
    bits = []
    b = n_dp // 2
    while b:
        bits.append(b)
        b //= 2
    lead = blocks[0]
    for b in bits:
        blocks = blocks + [over(a, "dp", b) for a in blocks]
        offs = offs + [o ^ b for o in offs]
    if early[1]:
        g1, u1 = prefetch(lead, [gate, up], [early[1], early[2]])
        held += [g1, u1]
        parts += [("g", early[1]), ("u", early[2])]

    late = 2 * experts - sum(len(p) for _, p in parts)
    x_bytes = all_rows * wide * 2
    with jax.named_scope("up"):
        h, slots = call(
            functools.partial(up_kernel, n_dp, parts),
            (
                jax.ShapeDtypeStruct((experts, all_rows, part), BF),
                jax.ShapeDtypeStruct((all_rows, LANES), BF),
            ),
            (*blocks, *[in_vmem(a) for a in held], in_hbm(gate), in_hbm(up)),
            [VM] * (n_dp + len(held)) + [HB, HB],
            (8 << 20) + 3 * x_bytes + late * size_of(gate) // experts,
            scratch=(
                pltpu.VMEM((late,) + gate.shape[1:], BF),
                pltpu.SemaphoreType.DMA((late,)),
            ),
        )

    chunks = [h]
    for b in bits:
        chunks = chunks + [over(a, "dp", b) for a in chunks]
    shrink2 = shrink.reshape(-1, shrink.shape[-1])
    expand2 = expand.reshape(-1, expand.shape[-1])
    every = list(range(experts))
    (down_v,) = prefetch(h, [down], [every])
    h_bytes = experts * all_rows * n_dp * max(part, LANES) * 2
    with jax.named_scope("down"):
        keep, send = call(
            functools.partial(down_kernel, offs, block),
            (
                jax.ShapeDtypeStruct((all_rows // 2, width), F32),
                jax.ShapeDtypeStruct((all_rows // 2, width), BF),
            ),
            (*chunks, slots, in_vmem(down_v), shrink2, expand2),
            [VM] * (n_dp + 4),
            (8 << 20) + 3 * h_bytes + all_rows * width * 4,
            scratch=(pltpu.VMEM((n_dp, experts, all_rows, part), BF),),
        )

    for b in bits[::-1][:-1]:
        arrived = over(send, "dp", b)
        half = keep.shape[0] // 2
        keep, send = call(
            halve,
            (
                jax.ShapeDtypeStruct((half, width), F32),
                jax.ShapeDtypeStruct((half, width), BF),
            ),
            (keep, arrived),
            [VM, VM],
            roomy + 4 * size_of(keep),
        )
    arrived = over(send, "dp", bits[0])
    own, *sends = call(
        functools.partial(split_rows, rows),
        (
            jax.ShapeDtypeStruct((rows, width), F32),
            *[jax.ShapeDtypeStruct((rows, width), BF) for _ in range(1, n_z)],
        ),
        (keep, arrived),
        [VM, VM],
        roomy + 4 * size_of(keep),
    )
    back = [over(s, "expert", k + 1) for k, s in enumerate(sends)]
    return call(
        finish,
        jax.ShapeDtypeStruct((rows, width), BF),
        (own, *back),
        [VM] * n_z,
        roomy,
    )


def solution(mesh):
    rows = ("group", "expert", "dp")
    in_specs = (
        P(rows, None),
        P(rows, None),
        P(rows, None),
        P(rows),
        P("expert", None, "dp"),
        P("expert", None, "dp"),
        P("expert", None, "dp"),
        P("expert", "dp", None, None),
        P("expert", "dp", None, None),
        P(),
        P(),
    )
    return jax.shard_map(
        shards, mesh=mesh, in_specs=in_specs, out_specs=P(rows, None), check_vma=False
    )
```

```python
import functools

import jax
import jax.numpy as jnp
from jax import lax
from jax.experimental import pallas as pl
from jax.experimental.pallas import tpu as pltpu
from jax.sharding import PartitionSpec as P

TOP = 8
EXPERTS = 16
SLOTS = 2
LANES = 128
BF = jnp.bfloat16
F32 = jnp.float32

VM = pl.BlockSpec(memory_space=pltpu.VMEM)
HB = pl.BlockSpec(memory_space=pltpu.HBM)


def in_vmem(x):
    return pltpu.with_memory_space_constraint(x, pltpu.VMEM)


def in_hbm(x):
    return pltpu.with_memory_space_constraint(x, pltpu.HBM)


def call(body, out_shape, operands, specs, limit, bytes_moved=0, scratch=()):
    return pl.pallas_call(
        body,
        out_shape=out_shape,
        in_specs=specs,
        out_specs=jax.tree.map(lambda _: VM, out_shape),
        scratch_shapes=scratch,
        cost_estimate=pl.CostEstimate(flops=0, bytes_accessed=bytes_moved, transcendentals=0),
        compiler_params=pltpu.CompilerParams(vmem_limit_bytes=limit),
    )(*operands)


def size_of(*arrays):
    total = 0
    for a in arrays:
        n = a.dtype.itemsize
        for s in a.shape[:-1]:
            n *= s
        total += n * (-(-a.shape[-1] // LANES) * LANES)
    return total


def prepare(*refs):
    y, held, sems = refs[9], refs[10:16], refs[16]
    copies = [pltpu.make_async_copy(refs[i], held[i], sems.at[i]) for i in range(6)]
    for c in copies:
        c.start()
    for c in copies:
        c.wait()
    ten, tok, ids, rw, owner, slot = held
    rows, width = tok.shape
    y[:, :width] = tok[...]
    lane = lax.broadcasted_iota(jnp.int32, (rows, LANES), 1)
    expert, piece = lane & (EXPERTS - 1), lane >> (EXPERTS.bit_length() - 1)
    w = jnp.zeros((rows, LANES), F32)
    for k in range(TOP):
        w += jnp.where(ids[:, k : k + 1] == expert, rw[:, k : k + 1], 0.0)
    high = w.astype(BF).astype(F32)
    mid = (w - high).astype(BF).astype(F32)
    low = w - high - mid
    y[:, width : width + LANES] = jnp.where(
        piece == 0, high, jnp.where(piece == 1, mid, jnp.where(piece == 2, low, 0.0))
    ).astype(BF)
    y[:, width + LANES :] = jnp.zeros((rows, LANES), BF)
    pages = [
        owner[pl.ds(ten[r], 1), :] * SLOTS + slot[pl.ds(ten[r], 1), :] for r in range(rows)
    ]
    y[:, width + LANES : width + LANES + EXPERTS] = (
        jnp.concatenate(pages, axis=0).astype(F32).astype(BF)
    )


def join(count, *refs):
    out = refs[-1]
    out[...] = jnp.concatenate([r[...].astype(F32) for r in refs[:count]], axis=0).astype(BF)


def up_kernel(count, *refs):
    x_refs = refs[:count]
    gate, up, h, slots, xs = refs[count:]
    experts, width = gate.shape[0], gate.shape[1]
    first = lax.axis_index("expert") * experts
    block = x_refs[0].shape[0]
    for i, r in enumerate(x_refs):
        xs[i * block : (i + 1) * block] = r[:, :width]
    meta = jnp.concatenate([r[:, width : width + LANES] for r in x_refs], axis=0).astype(F32)
    slots[...] = jnp.concatenate([r[:, width + LANES :] for r in x_refs], axis=0)
    lane = lax.broadcasted_iota(jnp.int32, meta.shape, 1)
    step = 256
    for e in range(experts):
        w = jnp.sum(
            jnp.where(lane & (EXPERTS - 1) == first + e, meta, 0.0), axis=1, keepdims=True
        )
        a = b = 0.0
        for k in range(0, width, step):
            x = xs[:, k : k + step]
            a += jnp.dot(x, gate[e, k : k + step], preferred_element_type=F32)
            b += jnp.dot(x, up[e, k : k + step], preferred_element_type=F32)
        h[e] = (a * jax.nn.sigmoid(a) * b * w).astype(BF)


def down_kernel(offs, block, *refs):
    n = len(offs)
    h_refs, refs = refs[:n], refs[n:]
    slots_ref, down, shrink, expand, keep, send, hs = refs
    me = lax.axis_index("dp")
    experts, rows, part = h_refs[0].shape
    first = lax.axis_index("expert") * experts
    for i, m in enumerate(offs):
        for p in range(n):
            q = offs.index(offs[p] ^ m)
            hs[me ^ m, :, p * block : (p + 1) * block, :] = h_refs[i][
                :, q * block : (q + 1) * block, :
            ]
    per = shrink.shape[0] // experts
    rank = per // SLOTS
    slot_values = slots_ref[...].astype(F32)
    lane16 = lax.broadcasted_iota(jnp.int32, slot_values.shape, 1)
    lane = lax.broadcasted_iota(jnp.int32, (rows, shrink.shape[0]), 1)
    wanted = me * SLOTS + (lane % per) // rank
    base = None
    small = jnp.zeros((rows, shrink.shape[0]), F32)
    joined = part % LANES == 0
    for e in range(experts):
        chosen = jnp.sum(
            jnp.where(lane16 == first + e, slot_values, 0.0), axis=1, keepdims=True
        ).astype(jnp.int32)
        pieces = [hs[c, e] for c in range(n)]
        cuts = [(c * part, (c + 1) * part) for c in range(n)]
        if joined:
            pieces, cuts = [jnp.concatenate(pieces, axis=1)], [(0, n * part)]
        full = jnp.zeros((rows, shrink.shape[0]), F32)
        for x, (lo, hi) in zip(pieces, cuts):
            term = jnp.dot(x, down[e, lo:hi, :], preferred_element_type=F32)
            base = term if base is None else base + term
            full += lax.dot_general(
                x, shrink[:, lo:hi], (((1,), (1,)), ((), ())), preferred_element_type=F32
            )
        small = jnp.where((lane // per == e) & (chosen == wanted), full, small)
    small = small.astype(BF)
    cols = base.shape[1]
    half = rows // 2
    for c in range(n):
        here = slice(c * cols, (c + 1) * cols)
        out = jnp.dot(small, expand[:, here], preferred_element_type=F32)
        out += jnp.where(me == c, base, 0.0)
        keep[:, here] = out[:half]
        send[:, here] = out[half:].astype(BF)


def halve(keep, got, new_keep, new_send):
    total = keep[...] + got[...].astype(F32)
    half = total.shape[0] // 2
    new_keep[...] = total[:half]
    new_send[...] = total[half:].astype(BF)


def split_rows(block, keep, got, own, *sends):
    total = keep[...] + got[...].astype(F32)
    own[...] = total[:block]
    for i, s in enumerate(sends):
        s[...] = total[(i + 1) * block : (i + 2) * block].astype(BF)


def finish(own, *refs):
    total = own[...]
    for r in refs[:-1]:
        total += r[...].astype(F32)
    refs[-1][...] = total.astype(BF)


def shards(tokens, expert_ids, route_weight, tenant_ids, gate, up, down, shrink, expand, owner, slot):
    n_z, n_dp = lax.axis_size("expert"), lax.axis_size("dp")
    rows, width = tokens.shape
    experts, _, part = gate.shape
    wide = width + 2 * LANES
    all_rows = rows * n_z * n_dp
    block = rows * n_z

    def over(x, axis, m):
        size = lax.axis_size(axis)
        return lax.ppermute(x, axis, [(i, i ^ m) for i in range(size)])

    roomy = 16 << 20
    inputs = (tenant_ids, tokens, expert_ids, route_weight, owner, slot)
    with jax.named_scope("prepare"):
        y = call(
            prepare,
            jax.ShapeDtypeStruct((rows, wide), BF),
            [in_hbm(a) for a in (*inputs, gate, up, down)],
            [HB] * (len(inputs) + 3),
            roomy,
            scratch=[
                *[(pltpu.VMEM if i else pltpu.SMEM)(a.shape, a.dtype) for i, a in enumerate(inputs)],
                pltpu.SemaphoreType.DMA((len(inputs),)),
            ],
        )

    got = [over(y, "expert", k) for k in range(1, n_z)]
    blocks = [
        call(
            functools.partial(join, n_z),
            jax.ShapeDtypeStruct((block, wide), BF),
            (y, *got),
            [VM] * n_z,
            roomy,
        )
    ]
    offs = [0]
    bits = []
    b = n_dp // 2
    while b:
        bits.append(b)
        b //= 2
    for b in bits:
        blocks = blocks + [over(a, "dp", b) for a in blocks]
        offs = offs + [o ^ b for o in offs]
    x_bytes = all_rows * wide * 2
    with jax.named_scope("up"):
        h, slots = call(
            functools.partial(up_kernel, n_dp),
            (
                jax.ShapeDtypeStruct((experts, all_rows, part), BF),
                jax.ShapeDtypeStruct((all_rows, LANES), BF),
            ),
            (*blocks, in_vmem(gate), in_vmem(up)),
            [VM] * n_dp + [VM, VM],
            (8 << 20) + 3 * x_bytes,
            scratch=(pltpu.VMEM((all_rows, width), BF),),
        )

    chunks = [h]
    for b in bits:
        chunks = chunks + [over(a, "dp", b) for a in chunks]
    shrink2 = shrink.reshape(-1, shrink.shape[-1])
    expand2 = expand.reshape(-1, expand.shape[-1])
    h_bytes = experts * all_rows * n_dp * max(part, LANES) * 2
    with jax.named_scope("down"):
        keep, send = call(
            functools.partial(down_kernel, offs, block),
            (
                jax.ShapeDtypeStruct((all_rows // 2, width), F32),
                jax.ShapeDtypeStruct((all_rows // 2, width), BF),
            ),
            (*chunks, slots, in_vmem(down), shrink2, expand2),
            [VM] * (n_dp + 4),
            (8 << 20) + 3 * h_bytes + all_rows * width * 4,
            scratch=(pltpu.VMEM((n_dp, experts, all_rows, part), BF),),
        )

    for b in bits[::-1][:-1]:
        arrived = over(send, "dp", b)
        half = keep.shape[0] // 2
        keep, send = call(
            halve,
            (
                jax.ShapeDtypeStruct((half, width), F32),
                jax.ShapeDtypeStruct((half, width), BF),
            ),
            (keep, arrived),
            [VM, VM],
            roomy + 4 * size_of(keep),
        )
    arrived = over(send, "dp", bits[0])
    own, *sends = call(
        functools.partial(split_rows, rows),
        (
            jax.ShapeDtypeStruct((rows, width), F32),
            *[jax.ShapeDtypeStruct((rows, width), BF) for _ in range(1, n_z)],
        ),
        (keep, arrived),
        [VM, VM],
        roomy + 4 * size_of(keep),
    )
    back = [over(s, "expert", k + 1) for k, s in enumerate(sends)]
    return call(
        finish,
        jax.ShapeDtypeStruct((rows, width), BF),
        (own, *back),
        [VM] * n_z,
        roomy,
    )


def solution(mesh):
    rows = ("group", "expert", "dp")
    in_specs = (
        P(rows, None),
        P(rows, None),
        P(rows, None),
        P(rows),
        P("expert", None, "dp"),
        P("expert", None, "dp"),
        P("expert", None, "dp"),
        P("expert", "dp", None, None),
        P("expert", "dp", None, None),
        P(),
        P(),
    )
    return jax.shard_map(
        shards, mesh=mesh, in_specs=in_specs, out_specs=P(rows, None), check_vma=False
    )
```

```python
import functools

import jax
import jax.numpy as jnp
from jax import lax
from jax.experimental import pallas as pl
from jax.experimental.pallas import tpu as pltpu
from jax.sharding import PartitionSpec as P

TOP = 8
EXPERTS = 16
SLOTS = 2
LANES = 128
BF = jnp.bfloat16
F32 = jnp.float32

VM = pl.BlockSpec(memory_space=pltpu.VMEM)
HB = pl.BlockSpec(memory_space=pltpu.HBM)


def in_vmem(x):
    return pltpu.with_memory_space_constraint(x, pltpu.VMEM)


def in_hbm(x):
    return pltpu.with_memory_space_constraint(x, pltpu.HBM)


def call(body, out_shape, operands, specs, limit, bytes_moved=0, scratch=()):
    return pl.pallas_call(
        body,
        out_shape=out_shape,
        in_specs=specs,
        out_specs=jax.tree.map(lambda _: VM, out_shape),
        scratch_shapes=scratch,
        cost_estimate=pl.CostEstimate(flops=0, bytes_accessed=bytes_moved, transcendentals=0),
        compiler_params=pltpu.CompilerParams(vmem_limit_bytes=limit),
    )(*operands)


def size_of(*arrays):
    total = 0
    for a in arrays:
        n = a.dtype.itemsize
        for s in a.shape[:-1]:
            n *= s
        total += n * (-(-a.shape[-1] // LANES) * LANES)
    return total


def prepare(*refs):
    y, held, sems = refs[9], refs[10:16], refs[16]
    copies = [pltpu.make_async_copy(refs[i], held[i], sems.at[i]) for i in range(6)]
    for c in copies:
        c.start()
    for c in copies:
        c.wait()
    ten, tok, ids, rw, owner, slot = held
    rows, width = tok.shape
    y[:, :width] = tok[...]
    lane = lax.broadcasted_iota(jnp.int32, (rows, LANES), 1)
    expert, piece = lane & (EXPERTS - 1), lane >> (EXPERTS.bit_length() - 1)
    w = jnp.zeros((rows, LANES), F32)
    for k in range(TOP):
        w += jnp.where(ids[:, k : k + 1] == expert, rw[:, k : k + 1], 0.0)
    high = w.astype(BF).astype(F32)
    mid = (w - high).astype(BF).astype(F32)
    low = w - high - mid
    y[:, width : width + LANES] = jnp.where(
        piece == 0, high, jnp.where(piece == 1, mid, jnp.where(piece == 2, low, 0.0))
    ).astype(BF)
    y[:, width + LANES :] = jnp.zeros((rows, LANES), BF)
    pages = [
        owner[pl.ds(ten[r], 1), :] * SLOTS + slot[pl.ds(ten[r], 1), :] for r in range(rows)
    ]
    y[:, width + LANES : width + LANES + EXPERTS] = (
        jnp.concatenate(pages, axis=0).astype(F32).astype(BF)
    )


def join(count, *refs):
    out = refs[-1]
    out[...] = jnp.concatenate([r[...].astype(F32) for r in refs[:count]], axis=0).astype(BF)


def relay(x, *refs):
    refs[-1][...] = x[...]


def up_kernel(count, picked, *refs):
    x_refs = refs[:count]
    gate, up, h, slots, xs = refs[count:]
    experts, width = gate.shape[0], gate.shape[1]
    first = lax.axis_index("expert") * experts
    block = x_refs[0].shape[0]
    for i, r in enumerate(x_refs):
        xs[i * block : (i + 1) * block] = r[:, :width]
    meta = jnp.concatenate([r[:, width : width + LANES] for r in x_refs], axis=0).astype(F32)
    slots[...] = jnp.concatenate([r[:, width + LANES :] for r in x_refs], axis=0)
    lane = lax.broadcasted_iota(jnp.int32, meta.shape, 1)
    step = 256
    for i, e in enumerate(picked):
        w = jnp.sum(
            jnp.where(lane & (EXPERTS - 1) == first + e, meta, 0.0), axis=1, keepdims=True
        )
        a = b = 0.0
        for k in range(0, width, step):
            x = xs[:, k : k + step]
            a += jnp.dot(x, gate[e, k : k + step], preferred_element_type=F32)
            b += jnp.dot(x, up[e, k : k + step], preferred_element_type=F32)
        h[i] = (a * jax.nn.sigmoid(a) * b * w).astype(BF)


def columns(ref, spot, size):
    if size % LANES == 0:
        return ref[:, pl.ds(pl.multiple_of(spot * size, size), size)]
    picked = ref[:, :size]
    for c in range(1, ref.shape[1] // size):
        picked = jnp.where(spot == c, ref[:, c * size : (c + 1) * size], picked)
    return picked


def down_kernel(offs, block, terms, opens, closes, *refs):
    n = len(offs)
    pairs, refs = refs[: 2 * len(terms)], refs[2 * len(terms) :]
    down, shrink, refs = refs[0], refs[1], refs[2:]
    base = small = None
    if not opens:
        base, small, refs = refs[0][...], refs[1][...], refs[2:]
    me = lax.axis_index("dp")
    odd = lax.rem(me, 2) == 1
    experts, part = down.shape[0], pairs[0].shape[2]
    rows, ranks = pairs[0].shape[1], shrink.shape[0]
    per = ranks // experts
    lane = lax.broadcasted_iota(jnp.int32, (rows, ranks), 1)

    def ordered(ref, i, m):
        cuts = [offs.index(o ^ m) * block for o in offs]
        return jnp.concatenate([ref[i, c : c + block, :] for c in cuts], axis=0)

    for t, (m, picked) in enumerate(terms):
        pair = (me ^ m) // 2
        for i, e in enumerate(picked):
            mine, other = ordered(pairs[2 * t], i, m), ordered(pairs[2 * t + 1], i, m ^ 1)
            x = [jnp.where(odd, other, mine), jnp.where(odd, mine, other)]
            if part % LANES == 0:
                x = [jnp.concatenate(x, axis=1)]
            for j, piece in enumerate(x):
                spot, size = pair * len(x) + j, piece.shape[1]
                here = pl.ds(pl.multiple_of(spot * size, size), size)
                term = jnp.dot(piece, down[e, here, :], preferred_element_type=F32)
                base = term if base is None else base + term
                term = lax.dot_general(
                    piece,
                    columns(shrink, spot, size),
                    (((1,), (1,)), ((), ())),
                    preferred_element_type=F32,
                )
                inside = (lane >= e * per) & (lane < (e + 1) * per)
                term = jnp.where(inside, term, 0.0)
                small = term if small is None else small + term
    if not closes:
        refs[0][...] = base
        refs[1][...] = small
        return
    slots, expand, keep, send = refs
    first = lax.axis_index("expert") * experts
    values = slots[...].astype(F32)
    lane16 = lax.broadcasted_iota(jnp.int32, values.shape, 1)
    rank = per // SLOTS
    chosen = jnp.full((rows, ranks), -1.0, F32)
    for e in range(experts):
        value = jnp.sum(jnp.where(lane16 == first + e, values, 0.0), axis=1, keepdims=True)
        for s in range(SLOTS):
            low_lane = e * per + s * rank
            inside = (lane >= low_lane) & (lane < low_lane + rank)
            mine = (me * SLOTS + s).astype(F32)
            chosen = jnp.where(inside, value - mine, chosen)
    small = jnp.where(chosen == 0.0, small, 0.0).astype(BF)
    cols = base.shape[1]
    half = rows // 2
    for c in range(n):
        here = slice(c * cols, (c + 1) * cols)
        out = jnp.dot(small, expand[:, here], preferred_element_type=F32)
        out += jnp.where(me == c, base, 0.0)
        keep[:, here] = out[:half]
        send[:, here] = out[half:].astype(BF)


def halve(keep, got, new_keep, new_send):
    total = keep[...] + got[...].astype(F32)
    half = total.shape[0] // 2
    new_keep[...] = total[:half]
    new_send[...] = total[half:].astype(BF)


def split_rows(block, keep, got, own, *sends):
    total = keep[...] + got[...].astype(F32)
    own[...] = total[:block]
    for i, s in enumerate(sends):
        s[...] = total[(i + 1) * block : (i + 2) * block].astype(BF)


def finish(own, *refs):
    total = own[...]
    for r in refs[:-1]:
        total += r[...].astype(F32)
    refs[-1][...] = total.astype(BF)


def shards(tokens, expert_ids, route_weight, tenant_ids, gate, up, down, shrink, expand, owner, slot):
    n_z, n_dp = lax.axis_size("expert"), lax.axis_size("dp")
    rows, width = tokens.shape
    experts, _, part = gate.shape
    wide = width + 2 * LANES
    all_rows = rows * n_z * n_dp
    block = rows * n_z

    def over(x, axis, m):
        size = lax.axis_size(axis)
        return lax.ppermute(x, axis, [(i, i ^ m) for i in range(size)])

    def passed(x, behind):
        return call(
            relay,
            jax.ShapeDtypeStruct(x.shape, x.dtype),
            (x, *behind),
            [VM] * (1 + len(behind)),
            roomy + 2 * size_of(x, *behind),
        )

    roomy = 16 << 20
    inputs = (tenant_ids, tokens, expert_ids, route_weight, owner, slot)
    with jax.named_scope("prepare"):
        y = call(
            prepare,
            jax.ShapeDtypeStruct((rows, wide), BF),
            [in_hbm(a) for a in (*inputs, gate, up, down)],
            [HB] * (len(inputs) + 3),
            roomy,
            scratch=[
                *[(pltpu.VMEM if i else pltpu.SMEM)(a.shape, a.dtype) for i, a in enumerate(inputs)],
                pltpu.SemaphoreType.DMA((len(inputs),)),
            ],
        )

    got = [over(y, "expert", k) for k in range(1, n_z)]
    blocks = [
        call(
            functools.partial(join, n_z),
            jax.ShapeDtypeStruct((block, wide), BF),
            (y, *got, in_hbm(gate), in_hbm(up), in_hbm(down)),
            [VM] * n_z + [HB] * 3,
            roomy,
        )
    ]
    offs = [0]
    bits = []
    b = n_dp // 2
    while b:
        bits.append(b)
        b //= 2
    for b in bits:
        blocks = blocks + [over(a, "dp", b) for a in blocks]
        offs = offs + [o ^ b for o in offs]
    x_bytes = all_rows * wide * 2
    lists = [list(range(experts))]
    if experts > 1:
        lists = [lists[0][: experts // 2], lists[0][experts // 2 :]]
    hidden = []
    for picked in lists:
        with jax.named_scope("up"):
            h, slots = call(
                functools.partial(up_kernel, n_dp, picked),
                (
                    jax.ShapeDtypeStruct((len(picked), all_rows, part), BF),
                    jax.ShapeDtypeStruct((all_rows, LANES), BF),
                ),
                (*blocks, in_vmem(gate), in_vmem(up)),
                [VM] * (n_dp + 2),
                (8 << 20) + 3 * x_bytes,
                scratch=(pltpu.VMEM((all_rows, width), BF),),
            )
        hidden.append({0: h})
    for b in bits[:-1]:
        for got in hidden:
            got.update({m ^ b: over(a, "dp", b) for m, a in got.items()})

    def between_cores(got, pairs, behind=()):
        for m in pairs:
            x = passed(got[m], behind) if behind else got[m]
            got[m ^ 1] = over(x, "dp", 1)

    others = list(range(2, n_dp, 2))
    for got in hidden:
        between_cores(got, [0] if got is hidden[-1] else [0, *others])

    shrink2 = shrink.reshape(-1, shrink.shape[-1])
    expand2 = expand.reshape(-1, expand.shape[-1])
    h_bytes = experts * all_rows * n_dp * max(part, LANES) * 2
    cols = down.shape[2]
    sums = (
        jax.ShapeDtypeStruct((all_rows, cols), F32),
        jax.ShapeDtypeStruct((all_rows, shrink2.shape[0]), F32),
    )
    halves = (
        jax.ShapeDtypeStruct((all_rows // 2, width), F32),
        jax.ShapeDtypeStruct((all_rows // 2, width), BF),
    )
    steps = [[(0, i) for i in range(len(lists))]]
    for i in range(len(lists)):
        steps.append([(m, i) for m in others])
    carried = ()
    for s, step in enumerate(steps):
        opens, closes = s == 0, s == len(steps) - 1
        if s == min(1, len(steps) - 1):
            between_cores(hidden[-1], others, carried)
        arrays = [a for m, i in step for a in (hidden[i][m], hidden[i][m ^ 1])]
        terms = [(m, lists[i]) for m, i in step]
        last = (slots, expand2) if closes else ()
        with jax.named_scope("down"):
            carried = call(
                functools.partial(down_kernel, offs, block, terms, opens, closes),
                halves if closes else sums,
                (*arrays, in_vmem(down), shrink2, *carried, *last),
                [VM] * (len(arrays) + 2 + len(carried) + len(last)),
                (8 << 20) + 2 * h_bytes + 2 * all_rows * width * 4,
            )
    keep, send = carried

    for b in bits[::-1][:-1]:
        arrived = over(send, "dp", b)
        half = keep.shape[0] // 2
        keep, send = call(
            halve,
            (
                jax.ShapeDtypeStruct((half, width), F32),
                jax.ShapeDtypeStruct((half, width), BF),
            ),
            (keep, arrived),
            [VM, VM],
            roomy + 4 * size_of(keep),
        )
    arrived = over(send, "dp", bits[0])
    own, *sends = call(
        functools.partial(split_rows, rows),
        (
            jax.ShapeDtypeStruct((rows, width), F32),
            *[jax.ShapeDtypeStruct((rows, width), BF) for _ in range(1, n_z)],
        ),
        (keep, arrived),
        [VM, VM],
        roomy + 4 * size_of(keep),
    )
    back = [over(sends[k - 1], "expert", k) for k in range(n_z - 1, 0, -1)]
    return call(
        finish,
        jax.ShapeDtypeStruct((rows, width), BF),
        (own, *back),
        [VM] * n_z,
        roomy,
    )


def solution(mesh):
    rows = ("group", "expert", "dp")
    in_specs = (
        P(rows, None),
        P(rows, None),
        P(rows, None),
        P(rows),
        P("expert", None, "dp"),
        P("expert", None, "dp"),
        P("expert", None, "dp"),
        P("expert", "dp", None, None),
        P("expert", "dp", None, None),
        P(),
        P(),
    )
    return jax.shard_map(
        shards, mesh=mesh, in_specs=in_specs, out_specs=P(rows, None), check_vma=False
    )
```

```python
import functools

import jax
import jax.numpy as jnp
from jax import lax
from jax.experimental import pallas as pl
from jax.experimental.pallas import tpu as pltpu
from jax.sharding import PartitionSpec as P

TOP = 8
EXPERTS = 16
SLOTS = 2
CAP = 3
LANES = 128
PIECES = 3
PARTS = 2
BF = jnp.bfloat16
F32 = jnp.float32

VM = pl.BlockSpec(memory_space=pltpu.VMEM)
HB = pl.BlockSpec(memory_space=pltpu.HBM)


def in_vmem(x):
    return pltpu.with_memory_space_constraint(x, pltpu.VMEM)


def in_hbm(x):
    return pltpu.with_memory_space_constraint(x, pltpu.HBM)


def shape(dims, dtype=BF):
    return jax.ShapeDtypeStruct(tuple(dims), dtype)


def size_of(*arrays):
    total = 0
    for a in arrays:
        n = jnp.dtype(a.dtype).itemsize
        for s in a.shape[:-1]:
            n *= s
        total += n * (-(-a.shape[-1] // LANES) * LANES)
    return total


def call(body, out_shape, operands, specs=None, room=2 << 20, scratch=()):
    specs = specs or [VM] * len(operands)
    held = [a for a, s in zip(operands, specs) if s is VM and size_of(a) < 1 << 20]
    limit = room + size_of(*held, *jax.tree.leaves(out_shape))
    return pl.pallas_call(
        body,
        out_shape=out_shape,
        in_specs=specs,
        out_specs=jax.tree.map(lambda _: VM, out_shape),
        scratch_shapes=scratch,
        cost_estimate=pl.CostEstimate(flops=0, bytes_accessed=0, transcendentals=0),
        compiler_params=pltpu.CompilerParams(vmem_limit_bytes=limit),
    )(*operands)


def prepare(*refs):
    ins, y, held, sems = refs[:6], refs[9], refs[10:16], refs[16]
    copies = [pltpu.make_async_copy(s, d, sems.at[i]) for i, (s, d) in enumerate(zip(ins, held))]
    for c in copies:
        c.start()
    for c in copies:
        c.wait()
    ten, tok, ids, rw, owner, slot = held
    rows, width = tok.shape
    y[:, :width] = tok[...]
    lane = lax.broadcasted_iota(jnp.int32, (rows, LANES), 1)
    expert, piece = lane & (EXPERTS - 1), lane >> (EXPERTS.bit_length() - 1)
    w = jnp.zeros((rows, LANES), F32)
    routed = jnp.zeros((rows, LANES), F32)
    for k in range(TOP):
        same = ids[:, k : k + 1] == expert
        w += jnp.where(same, rw[:, k : k + 1], 0.0)
        routed += jnp.where(same, 1.0, 0.0)
    places = [routed[:1]]
    for r in range(1, rows):
        places.append(places[-1] + routed[r : r + 1])
    place = jnp.concatenate(places, axis=0) * routed
    high = w.astype(BF).astype(F32)
    mid = (w - high).astype(BF).astype(F32)
    low = w - high - mid
    block = jnp.zeros((rows, LANES), F32)
    for i, value in enumerate((high, mid, low, place)):
        block = jnp.where(piece == i, value, block)
    y[:, width : width + LANES] = block.astype(BF)
    y[:, width + LANES :] = jnp.zeros((rows, LANES), BF)
    pages = [
        owner[pl.ds(ten[r], 1), :] * SLOTS + slot[pl.ds(ten[r], 1), :] for r in range(rows)
    ]
    y[:, width + LANES : width + LANES + EXPERTS] = (
        jnp.concatenate(pages, axis=0).astype(F32).astype(BF)
    )


def join_blocks(count, *refs):
    parts = [r[...].astype(F32) for r in refs[:count]]
    refs[-1][...] = jnp.concatenate(parts, axis=0).astype(BF)


def relay(x, *refs):
    refs[-1][...] = x[...]


def column(meta, lane, wanted):
    return jnp.sum(jnp.where(lane == wanted, meta, 0.0), axis=1, keepdims=True)


def picks(meta, lane, expert, each, flip):
    rows = meta.shape[0]
    place = column(meta, lane, PIECES * EXPERTS + expert).astype(jnp.int32)
    block = lax.broadcasted_iota(jnp.int32, (rows, 1), 0) >> (each.bit_length() - 1)
    target = jnp.where(place > 0, (block ^ flip) * CAP + place - 1, -1)
    slots = rows // each * CAP
    spot = lax.broadcasted_iota(jnp.int32, (rows, slots), 1)
    return jnp.where(spot == target, 1.0, 0.0).astype(BF)


def gather_rows(places, *refs):
    blocks, xs, info = refs[: len(places)], refs[-2], refs[-1]
    size, width = blocks[0].shape[0], xs.shape[1]
    in_order = [blocks[places.index(i)] for i in range(len(places))]
    for i in range(0, len(places), 2):
        pair = [r[...].astype(F32) for r in in_order[i : i + 2]]
        both = jnp.concatenate(pair, axis=0).astype(BF)
        xs[i * size : (i + 2) * size] = both[:, :width]
        info[i * size : (i + 2) * size] = both[:, width:]


def up_kernel(picked, each, *refs):
    xs, info, gate, up, h, packed = refs
    experts, width = gate.shape[0], gate.shape[1]
    first = lax.axis_index("expert") * experts
    meta = info[:, :LANES].astype(F32)
    lane = lax.broadcasted_iota(jnp.int32, meta.shape, 1)
    weight = jnp.where(lane < PIECES * EXPERTS, meta, 0.0)
    step = 256
    for i, e in enumerate(picked):
        w = column(weight, lane & (EXPERTS - 1), first + e)
        a = b = 0.0
        for k in range(0, width, step):
            x = xs[:, k : k + step]
            a += jnp.dot(x, gate[e, k : k + step], preferred_element_type=F32)
            b += jnp.dot(x, up[e, k : k + step], preferred_element_type=F32)
        hidden = (a * jax.nn.sigmoid(a) * b * w).astype(BF)
        h[i] = hidden
        packed[i] = lax.dot_general(
            picks(meta, lane, first + e, each, 0),
            hidden,
            (((0,), (0,)), ((), ())),
            preferred_element_type=F32,
        ).astype(BF)


def columns(ref, spot, size):
    if size % LANES == 0:
        return ref[:, pl.ds(pl.multiple_of(spot * size, size), size)]
    picked = ref[:, :size]
    for c in range(1, ref.shape[1] // size):
        picked = jnp.where(spot == c, ref[:, c * size : (c + 1) * size], picked)
    return picked


def down_kernel(each, n, flips, terms, opens, cut, *refs):
    pairs, refs = refs[: 2 * len(terms)], refs[2 * len(terms) :]
    (info, down, shrink), refs = refs[:3], refs[3:]
    base = small = spreads = here_ref = None
    if not opens:
        base, small, here_ref = refs[0][...], refs[1][...], refs[2]
        refs = refs[3:]
        if flips:
            spreads, refs = refs[0], refs[1:]
    me = lax.axis_index("dp")
    odd = lax.rem(me, 2) == 1
    experts = down.shape[0]
    part = pairs[0].shape[2]
    rows, ranks = info.shape[0], shrink.shape[0]
    half, per = rows // 2, ranks // experts
    cols = down.shape[2]
    across = slice(0, cols)
    if cut is not None:
        across = slice(cut * (cols // PARTS), (cut + 1) * (cols // PARTS))
        base = base[:, across]
    first = lax.axis_index("expert") * experts
    meta = info[:, :LANES].astype(F32)
    lane16 = lax.broadcasted_iota(jnp.int32, meta.shape, 1)
    lane = lax.broadcasted_iota(jnp.int32, (rows, ranks), 1)

    def spread(e, m):
        flip = (m & 1) * (half // each) + (m >> 1)
        return picks(meta, lane16, first + e, each, flip)

    def turned(m):
        flip = (m & 1) * (half // each) + (m >> 1)
        there = lax.broadcasted_iota(jnp.int32, (rows, rows), 0) ^ (flip * each)
        return jnp.where(lax.broadcasted_iota(jnp.int32, (rows, rows), 1) == there, 1.0, 0.0).astype(BF)

    def ordered(ref, i, e, m):
        if m == 0:
            return ref[i]
        if ref.shape[1] == rows:
            return jnp.dot(turned(m), ref[i], preferred_element_type=F32).astype(BF)
        known = spreads is not None and m in flips
        one_hot = spreads[flips.index(m) * experts + e] if known else spread(e, m)
        return jnp.dot(one_hot, ref[i], preferred_element_type=F32).astype(BF)

    for t, (m, picked) in enumerate(terms):
        pair = (me ^ m) // 2
        for i, e in enumerate(picked):
            mine = ordered(pairs[2 * t], i, e, m)
            other = ordered(pairs[2 * t + 1], i, e, m ^ 1)
            x = [jnp.where(odd, other, mine), jnp.where(odd, mine, other)]
            if part % LANES == 0:
                x = [jnp.concatenate(x, axis=1)]
            for j, piece in enumerate(x):
                spot, size = pair * len(x) + j, piece.shape[1]
                at = pl.ds(pl.multiple_of(spot * size, size), size)
                term = jnp.dot(piece, down[e, at, across], preferred_element_type=F32)
                base = term if base is None else base + term
                if cut:
                    continue
                term = lax.dot_general(
                    piece,
                    columns(shrink, spot, size),
                    (((1,), (1,)), ((), ())),
                    preferred_element_type=F32,
                )
                inside = (lane >= e * per) & (lane < (e + 1) * per)
                term = jnp.where(inside, term, 0.0)
                small = term if small is None else small + term
    if opens:
        refs[0][...] = base
        refs[1][...] = small
        values = info[:, LANES:].astype(F32)
        rank = per // SLOTS
        away = jnp.full((rows, ranks), -1.0, F32)
        for e in range(experts):
            value = column(values, lane16, first + e)
            for s in range(SLOTS):
                low = e * per + s * rank
                inside = (lane >= low) & (lane < low + rank)
                away = jnp.where(inside, value - (me * SLOTS + s).astype(F32), away)
        refs[2][...] = jnp.where(away == 0.0, 1.0, 0.0)
        for f, m in enumerate(flips):
            for e in range(experts):
                refs[3][f * experts + e] = spread(e, m)
        return
    if cut is None:
        refs[0][...] = base
        refs[1][...] = small
        return
    if cut == 0:
        expand, keep, send, ready = refs
        small = (small * here_ref[...]).astype(BF)
        ready[...] = small
    else:
        expand, ready, keep, send = refs
        small = ready[...]
    size = cols // PARTS
    for c in range(n):
        here = slice(c * size, (c + 1) * size)
        there = slice(c * cols + across.start, c * cols + across.stop)
        out = jnp.dot(small, expand[:, there], preferred_element_type=F32)
        out += jnp.where(me == c, base, 0.0)
        keep[:, here] = out[:half]
        send[:, here] = out[half:].astype(BF)


def add_and_deal(size, count, sets, *refs):
    ins, outs = refs[: count * sets], refs[count * sets :]
    width = ins[0].shape[1]
    for s in range(sets):
        total = ins[s * count][...]
        for r in ins[s * count + 1 : (s + 1) * count]:
            total += r[...].astype(F32)
        parts = [total[r : r + size] for r in range(0, total.shape[0], size)]
        for i, o in enumerate(outs):
            dealt = jnp.concatenate(parts[i :: len(outs)], axis=0)
            o[:, s * width : (s + 1) * width] = dealt.astype(o.dtype)


def finish(cols, *refs):
    total = refs[0][...]
    for r in refs[1:-1]:
        total += r[...].astype(F32)
    size, n = cols // PARTS, total.shape[1] // cols
    for p in range(PARTS):
        for c in range(n):
            at = (p * n + c) * size
            to = c * cols + p * size
            refs[-1][:, to : to + size] = total[:, at : at + size].astype(BF)


def shards(tokens, expert_ids, route_weight, tenant_ids, gate, up, down, shrink, expand, owner, slot):
    n_z, n_dp = lax.axis_size("expert"), lax.axis_size("dp")
    n_x = n_dp // 2
    rows, width = tokens.shape
    experts, _, part = gate.shape
    wide = width + 2 * LANES
    block = rows * n_x
    half_rows = block * n_z
    all_rows = 2 * half_rows
    x_bits = [b for b in (2, 4, 8, 16, 32, 64) if b < n_dp]

    def over(x, axis, m):
        return lax.ppermute(x, axis, [(i, i ^ m) for i in range(lax.axis_size(axis))])

    inputs = (tenant_ids, tokens, expert_ids, route_weight, owner, slot)
    weights = [in_hbm(a) for a in (gate, up, down)]
    with jax.named_scope("prepare"):
        y = call(
            prepare,
            shape((rows, wide)),
            [*[in_hbm(a) for a in inputs], *weights],
            [HB] * (len(inputs) + 3),
            scratch=[
                *[(pltpu.VMEM if i else pltpu.SMEM)(a.shape, a.dtype) for i, a in enumerate(inputs)],
                pltpu.SemaphoreType.DMA((len(inputs),)),
            ],
        )

    blocks = [y]
    for b in x_bits:
        blocks = blocks + [over(a, "dp", b) for a in blocks]
    with jax.named_scope("join"):
        lead = call(
            functools.partial(join_blocks, n_x),
            shape((block, wide)),
            (*blocks, *weights),
            [VM] * n_x + [HB] * 3,
            room=(2 << 20) + 4 * block * wide,
        )
    along_z = {k: over(lead, "expert", k) if k else lead for k in range(n_z)}
    places = [0, *range(n_z - 1, 0, -1)]
    places += [k + n_z for k in places]
    gathered = [along_z[k] for k in places[:n_z]]
    gathered += [over(a, "dp", 1) for a in gathered]

    lists = [list(range(experts))]
    if experts > 1:
        lists = [lists[0][: experts // 2], lists[0][experts // 2 :]]
    packed_rows = all_rows // rows * CAP
    with jax.named_scope("gather"):
        xs, info = call(
            functools.partial(gather_rows, places),
            [shape((all_rows, width)), shape((all_rows, 2 * LANES))],
            gathered,
        )
    hidden = []
    for picked in lists:
        with jax.named_scope("up"):
            h, packed = call(
                functools.partial(up_kernel, picked, rows),
                [
                    shape((len(picked), all_rows, part)),
                    shape((len(picked), packed_rows, part)),
                ],
                (xs, info, in_vmem(gate), in_vmem(up)),
                room=(4 << 20) + 4 * all_rows * (packed_rows + 4 * part + 8 * LANES),
            )
        hidden.append({0: h, "packed": packed})
    for got in hidden:
        moved = {0: got["packed"] if got is hidden[-1] else got[0]}
        for b in x_bits:
            moved.update({m | b: over(a, "dp", b) for m, a in moved.items()})
        got.update({m: a for m, a in moved.items() if m})

    def between_cores(got, pairs, behind=()):
        for m in pairs:
            x = got[m] if m else got["packed"]
            if behind:
                x = call(relay, shape(x.shape), (x, *behind))
            got[m ^ 1] = over(x, "dp", 1)

    others = list(range(2, n_dp, 2))
    for got in hidden:
        between_cores(got, [0] if got is hidden[-1] else [0, *others])

    shrink2 = shrink.reshape(-1, shrink.shape[-1])
    expand2 = expand.reshape(-1, expand.shape[-1])
    cols = down.shape[2]
    ranks = shrink2.shape[0]
    sums = [shape((all_rows, cols), F32), shape((all_rows, ranks), F32)]
    spreads = shape(((n_dp - 2) * experts, all_rows, packed_rows))
    flips = list(range(2, n_dp)) if size_of(spreads) < 1 << 20 else []
    steps = [[(0, i) for i in range(len(lists))]]
    steps += [[(m, i) for m in others] for i in range(len(lists))]
    carried, routing = [], []

    def add_terms(step, opens, cut, outs, after):
        arrays = [a for m, i in step for a in (hidden[i][m], hidden[i][m ^ 1])]
        terms = [(m, lists[i]) for m, i in step]
        with jax.named_scope("down"):
            return call(
                functools.partial(down_kernel, rows, n_dp, flips, terms, opens, cut),
                outs,
                [*arrays, *(info, in_vmem(down), shrink2), *carried, *routing, *after],
                room=(6 << 20) + 4 * all_rows * (4 * cols + 2 * packed_rows + 4 * part),
            )

    for s, step in enumerate(steps[:-1]):
        if s == 1:
            between_cores(hidden[-1], others, carried)
        outs = list(sums)
        if s == 0:
            outs += [shape((all_rows, ranks), F32)] + ([spreads] if flips else [])
        carried = add_terms(step, s == 0, None, outs, [])
        if s == 0:
            carried, routing = carried[:2], carried[2:]
    if len(steps) == 2:
        between_cores(hidden[-1], others, carried)

    some = width // PARTS
    arrived, after = [], [expand2]
    for cut in range(PARTS):
        outs = [shape((half_rows, some), F32), shape((half_rows, some))]
        ready = shape((all_rows, ranks))
        keep, send, *more = add_terms(
            steps[-1], False, cut, outs + ([ready] if cut == 0 else []), after
        )
        after = after + more
        terms, left = [keep, over(send, "dp", 1)], n_x
        for b in x_bits[::-1]:
            left //= 2
            dims = (n_z * left * rows, some)
            kept = call(
                functools.partial(add_and_deal, left * rows, 2, 1),
                [shape(dims, F32), shape(dims)],
                terms,
                room=(2 << 20) + 3 * size_of(terms[0]),
            )
            terms = [kept[0], over(kept[1], "dp", b)]
        arrived += terms
    kept = call(
        functools.partial(add_and_deal, rows, 2, PARTS),
        [shape((rows, width), F32)] + [shape((rows, width))] * (n_z - 1),
        arrived,
        room=(2 << 20) + 6 * size_of(arrived[0]),
    )
    back = [over(kept[k], "expert", k) for k in range(n_z - 1, 0, -1)]
    with jax.named_scope("finish"):
        return call(
            functools.partial(finish, cols),
            shape((rows, width)),
            [kept[0], *back],
        )


def solution(mesh):
    rows = ("group", "expert", "dp")
    in_specs = (
        P(rows, None),
        P(rows, None),
        P(rows, None),
        P(rows),
        P("expert", None, "dp"),
        P("expert", None, "dp"),
        P("expert", None, "dp"),
        P("expert", "dp", None, None),
        P("expert", "dp", None, None),
        P(),
        P(),
    )
    return jax.shard_map(
        shards, mesh=mesh, in_specs=in_specs, out_specs=P(rows, None), check_vma=False
    )
```

```python
import functools

import jax
import jax.numpy as jnp
from jax import lax
from jax.experimental import pallas as pl
from jax.experimental.pallas import tpu as pltpu
from jax.sharding import PartitionSpec as P

TOP = 8
EXPERTS = 16
SLOTS = 2
CAP = 3
LANES = 128
PIECES = 3
PARTS = 2
BF = jnp.bfloat16
F32 = jnp.float32

VM = pl.BlockSpec(memory_space=pltpu.VMEM)
HB = pl.BlockSpec(memory_space=pltpu.HBM)


def in_vmem(x):
    return pltpu.with_memory_space_constraint(x, pltpu.VMEM)


def in_hbm(x):
    return pltpu.with_memory_space_constraint(x, pltpu.HBM)


def shape(dims, dtype=BF):
    return jax.ShapeDtypeStruct(tuple(dims), dtype)


def size_of(*arrays):
    total = 0
    for a in arrays:
        n = jnp.dtype(a.dtype).itemsize
        for s in a.shape[:-1]:
            n *= s
        total += n * (-(-a.shape[-1] // LANES) * LANES)
    return total


def call(body, out_shape, operands, specs=None, room=2 << 20, scratch=()):
    specs = specs or [VM] * len(operands)
    held = [a for a, s in zip(operands, specs) if s is VM and size_of(a) < 1 << 20]
    limit = room + size_of(*held, *jax.tree.leaves(out_shape))
    return pl.pallas_call(
        body,
        out_shape=out_shape,
        in_specs=specs,
        out_specs=jax.tree.map(lambda _: VM, out_shape),
        scratch_shapes=scratch,
        cost_estimate=pl.CostEstimate(flops=0, bytes_accessed=0, transcendentals=0),
        compiler_params=pltpu.CompilerParams(vmem_limit_bytes=limit),
    )(*operands)


def prepare(*refs):
    ins, y, held, sems = refs[:6], refs[9], refs[10:16], refs[16]
    copies = [pltpu.make_async_copy(s, d, sems.at[i]) for i, (s, d) in enumerate(zip(ins, held))]
    for c in copies:
        c.start()
    for c in copies:
        c.wait()
    ten, tok, ids, rw, owner, slot = held
    rows, width = tok.shape
    y[:, :width] = tok[...]
    lane = lax.broadcasted_iota(jnp.int32, (rows, LANES), 1)
    expert, piece = lane & (EXPERTS - 1), lane >> (EXPERTS.bit_length() - 1)
    w = jnp.zeros((rows, LANES), F32)
    routed = jnp.zeros((rows, LANES), F32)
    for k in range(TOP):
        same = ids[:, k : k + 1] == expert
        w += jnp.where(same, rw[:, k : k + 1], 0.0)
        routed += jnp.where(same, 1.0, 0.0)
    places = [routed[:1]]
    for r in range(1, rows):
        places.append(places[-1] + routed[r : r + 1])
    place = jnp.concatenate(places, axis=0) * routed
    high = w.astype(BF).astype(F32)
    mid = (w - high).astype(BF).astype(F32)
    low = w - high - mid
    pages = [
        owner[pl.ds(ten[r], 1), :] * SLOTS + slot[pl.ds(ten[r], 1), :] for r in range(rows)
    ]
    slots = jnp.concatenate(pages, axis=0).astype(F32)
    block = jnp.concatenate([slots] * (LANES // EXPERTS), axis=1)
    for i, value in enumerate((high, mid, low, place)):
        block = jnp.where(piece == i, value, block)
    y[:, width:] = block.astype(BF)


def join_blocks(count, *refs):
    parts = [r[...].astype(F32) for r in refs[:count]]
    refs[-1][...] = jnp.concatenate(parts, axis=0).astype(BF)


def relay(x, *refs):
    refs[-1][...] = x[...]


def column(meta, lane, wanted):
    return jnp.sum(jnp.where(lane == wanted, meta, 0.0), axis=1, keepdims=True)


def picks(meta, lane, expert, each, flip):
    rows = meta.shape[0]
    place = column(meta, lane, PIECES * EXPERTS + expert).astype(jnp.int32)
    block = lax.broadcasted_iota(jnp.int32, (rows, 1), 0) >> (each.bit_length() - 1)
    target = jnp.where(place > 0, (block ^ flip) * CAP + place - 1, -1)
    slots = rows // each * CAP
    spot = lax.broadcasted_iota(jnp.int32, (rows, slots), 1)
    return jnp.where(spot == target, 1.0, 0.0).astype(BF)


def gather_rows(places, *refs):
    blocks, xs, info = refs[: len(places)], refs[-2], refs[-1]
    size, width = blocks[0].shape[0], xs.shape[1]
    in_order = [blocks[places.index(i)] for i in range(len(places))]
    for i in range(0, len(places), 2):
        pair = [r[...].astype(F32) for r in in_order[i : i + 2]]
        both = jnp.concatenate(pair, axis=0).astype(BF)
        xs[i * size : (i + 2) * size] = both[:, :width]
        info[i * size : (i + 2) * size] = both[:, width:]


def up_kernel(picked, each, *refs):
    xs, info, gate, up, h, *packed = refs
    experts, width = gate.shape[0], gate.shape[1]
    first = lax.axis_index("expert") * experts
    meta = info[...].astype(F32)
    lane = lax.broadcasted_iota(jnp.int32, meta.shape, 1)
    weight = jnp.where(lane < PIECES * EXPERTS, meta, 0.0)
    step = 256
    for i, e in enumerate(picked):
        w = column(weight, lane & (EXPERTS - 1), first + e)
        a = b = 0.0
        for k in range(0, width, step):
            x = xs[:, k : k + step]
            a += jnp.dot(x, gate[e, k : k + step], preferred_element_type=F32)
            b += jnp.dot(x, up[e, k : k + step], preferred_element_type=F32)
        hidden = (a * jax.nn.sigmoid(a) * b * w).astype(BF)
        h[i] = hidden
        if not packed:
            continue
        packed[0][i] = lax.dot_general(
            picks(meta, lane, first + e, each, 0),
            hidden,
            (((0,), (0,)), ((), ())),
            preferred_element_type=F32,
        ).astype(BF)


def columns(ref, spot, size):
    if size % LANES == 0:
        return ref[:, pl.ds(pl.multiple_of(spot * size, size), size)]
    picked = ref[:, :size]
    for c in range(1, ref.shape[1] // size):
        picked = jnp.where(spot == c, ref[:, c * size : (c + 1) * size], picked)
    return picked


def down_kernel(each, n, flips, terms, opens, cut, *refs):
    pairs, refs = refs[: 2 * len(terms)], refs[2 * len(terms) :]
    (info, down, shrink), refs = refs[:3], refs[3:]
    base = small = spreads = here_ref = None
    if not opens:
        base, small, here_ref = refs[0][...], refs[1][...], refs[2]
        refs = refs[3:]
        if flips:
            spreads, refs = refs[0], refs[1:]
    me = lax.axis_index("dp")
    odd = lax.rem(me, 2) == 1
    experts = down.shape[0]
    part = pairs[0].shape[2]
    rows, ranks = info.shape[0], shrink.shape[0]
    half, per = rows // 2, ranks // experts
    cols = down.shape[2]
    across = slice(0, cols)
    if cut is not None:
        across = slice(cut * (cols // PARTS), (cut + 1) * (cols // PARTS))
        base = base[:, across]
    first = lax.axis_index("expert") * experts
    meta = info[...].astype(F32)
    lane16 = lax.broadcasted_iota(jnp.int32, meta.shape, 1)
    lane = lax.broadcasted_iota(jnp.int32, (rows, ranks), 1)

    def spread(e, m):
        flip = (m & 1) * (half // each) + (m >> 1)
        return picks(meta, lane16, first + e, each, flip)

    def turned(m):
        flip = (m & 1) * (half // each) + (m >> 1)
        there = lax.broadcasted_iota(jnp.int32, (rows, rows), 0) ^ (flip * each)
        return jnp.where(lax.broadcasted_iota(jnp.int32, (rows, rows), 1) == there, 1.0, 0.0).astype(BF)

    def ordered(ref, i, e, m):
        if m == 0:
            return ref[i]
        if ref.shape[1] == rows and m == 1:
            return jnp.concatenate([ref[i, half:], ref[i, :half]], axis=0)
        if ref.shape[1] == rows:
            return jnp.dot(turned(m), ref[i], preferred_element_type=F32).astype(BF)
        known = spreads is not None and m in flips
        one_hot = spreads[flips.index(m) * experts + e] if known else spread(e, m)
        return jnp.dot(one_hot, ref[i], preferred_element_type=F32).astype(BF)

    for t, (m, picked) in enumerate(terms):
        pair = (me ^ m) // 2
        for i, e in enumerate(picked):
            mine = ordered(pairs[2 * t], i, e, m)
            other = ordered(pairs[2 * t + 1], i, e, m ^ 1)
            x = [jnp.where(odd, other, mine), jnp.where(odd, mine, other)]
            if part % LANES == 0:
                x = [jnp.concatenate(x, axis=1)]
            for j, piece in enumerate(x):
                spot, size = pair * len(x) + j, piece.shape[1]
                at = pl.ds(pl.multiple_of(spot * size, size), size)
                term = jnp.dot(piece, down[e, at, across], preferred_element_type=F32)
                base = term if base is None else base + term
                if cut:
                    continue
                term = lax.dot_general(
                    piece,
                    columns(shrink, spot, size),
                    (((1,), (1,)), ((), ())),
                    preferred_element_type=F32,
                )
                inside = (lane >= e * per) & (lane < (e + 1) * per)
                term = jnp.where(inside, term, 0.0)
                small = term if small is None else small + term
    if opens:
        refs[0][...] = base
        refs[1][...] = small
        rank = per // SLOTS
        away = jnp.full((rows, ranks), -1.0, F32)
        for e in range(experts):
            value = column(meta, lane16, (PIECES + 1) * EXPERTS + first + e)
            for s in range(SLOTS):
                low = e * per + s * rank
                inside = (lane >= low) & (lane < low + rank)
                away = jnp.where(inside, value - (me * SLOTS + s).astype(F32), away)
        refs[2][...] = jnp.where(away == 0.0, 1.0, 0.0)
        for f, m in enumerate(flips):
            for e in range(experts):
                refs[3][f * experts + e] = spread(e, m)
        return
    if cut is None:
        refs[0][...] = base
        refs[1][...] = small
        return
    if cut == 0:
        expand, keep, send, ready = refs
        small = (small * here_ref[...]).astype(BF)
        ready[...] = small
    else:
        expand, ready, keep, send = refs
        small = ready[...]
    size = cols // PARTS
    for c in range(n):
        here = slice(c * size, (c + 1) * size)
        there = slice(c * cols + across.start, c * cols + across.stop)
        out = jnp.dot(small, expand[:, there], preferred_element_type=F32)
        out += jnp.where(me == c, base, 0.0)
        keep[:, here] = out[:half]
        send[:, here] = out[half:].astype(BF)


def add_and_deal(size, count, sets, *refs):
    ins, outs = refs[: count * sets], refs[count * sets :]
    width = ins[0].shape[1]
    for s in range(sets):
        total = ins[s * count][...]
        for r in ins[s * count + 1 : (s + 1) * count]:
            total += r[...].astype(F32)
        parts = [total[r : r + size] for r in range(0, total.shape[0], size)]
        for i, o in enumerate(outs):
            dealt = jnp.concatenate(parts[i :: len(outs)], axis=0)
            o[:, s * width : (s + 1) * width] = dealt.astype(o.dtype)


def finish(cols, *refs):
    total = refs[0][...]
    for r in refs[1:-1]:
        total += r[...].astype(F32)
    size, n = cols // PARTS, total.shape[1] // cols
    for p in range(PARTS):
        for c in range(n):
            at = (p * n + c) * size
            to = c * cols + p * size
            refs[-1][:, to : to + size] = total[:, at : at + size].astype(BF)


def shards(tokens, expert_ids, route_weight, tenant_ids, gate, up, down, shrink, expand, owner, slot):
    n_z, n_dp = lax.axis_size("expert"), lax.axis_size("dp")
    n_x = n_dp // 2
    rows, width = tokens.shape
    experts, _, part = gate.shape
    wide = width + LANES
    block = rows * n_x
    half_rows = block * n_z
    all_rows = 2 * half_rows
    x_bits = [b for b in (2, 4, 8, 16, 32, 64) if b < n_dp]

    def over(x, axis, m):
        return lax.ppermute(x, axis, [(i, i ^ m) for i in range(lax.axis_size(axis))])

    inputs = (tenant_ids, tokens, expert_ids, route_weight, owner, slot)
    weights = [in_hbm(a) for a in (gate, up, down)]
    with jax.named_scope("prepare"):
        y = call(
            prepare,
            shape((rows, wide)),
            [*[in_hbm(a) for a in inputs], *weights],
            [HB] * (len(inputs) + 3),
            scratch=[
                *[(pltpu.VMEM if i else pltpu.SMEM)(a.shape, a.dtype) for i, a in enumerate(inputs)],
                pltpu.SemaphoreType.DMA((len(inputs),)),
            ],
        )

    blocks = [y]
    for b in x_bits:
        blocks = blocks + [over(a, "dp", b) for a in blocks]
    with jax.named_scope("join"):
        lead = call(
            functools.partial(join_blocks, n_x),
            shape((block, wide)),
            (*blocks, *weights),
            [VM] * n_x + [HB] * 3,
            room=(2 << 20) + 4 * block * wide,
        )
    along_z = {k: over(lead, "expert", k) if k else lead for k in range(n_z)}
    places = [0, *range(n_z - 1, 0, -1)]
    places += [k + n_z for k in places]
    gathered = [along_z[k] for k in places[:n_z]]
    gathered += [over(a, "dp", 1) for a in gathered]

    lists = [list(range(experts))]
    if experts > 1:
        lists = [lists[0][: experts // 2], lists[0][experts // 2 :]]
    packed_rows = all_rows // rows * CAP
    with jax.named_scope("gather"):
        xs, info = call(
            functools.partial(gather_rows, places),
            [shape((all_rows, width)), shape((all_rows, LANES))],
            gathered,
        )
    hidden = []
    for picked in lists:
        with jax.named_scope("up"):
            outs = [shape((len(picked), all_rows, part))]
            if picked is lists[-1]:
                outs.append(shape((len(picked), packed_rows, part)))
            h, *packed = call(
                functools.partial(up_kernel, picked, rows),
                outs,
                (xs, info, in_vmem(gate), in_vmem(up)),
                room=(4 << 20) + 4 * all_rows * (packed_rows + 4 * part + 8 * LANES),
            )
        hidden.append({0: h, "sent": packed[0] if packed else h})
    for got in hidden:
        moved = {0: got["sent"]}
        for b in x_bits:
            moved.update({m | b: over(a, "dp", b) for m, a in moved.items()})
        got.update({m: a for m, a in moved.items() if m})

    def between_cores(got, pairs, behind=()):
        for m in pairs:
            x = got[m] if m else got["sent"]
            if behind:
                x = call(relay, shape(x.shape), (x, *behind))
            got[m ^ 1] = over(x, "dp", 1)

    others = list(range(2, n_dp, 2))
    for got in hidden:
        between_cores(got, [0] if got is hidden[-1] else [0, *others])

    shrink2 = shrink.reshape(-1, shrink.shape[-1])
    expand2 = expand.reshape(-1, expand.shape[-1])
    cols = down.shape[2]
    ranks = shrink2.shape[0]
    sums = [shape((all_rows, cols), F32), shape((all_rows, ranks), F32)]
    spreads = shape(((n_dp - 2) * experts, all_rows, packed_rows))
    flips = list(range(2, n_dp)) if size_of(spreads) < 1 << 20 else []
    steps = [[(0, i) for i in range(len(lists))]]
    steps += [[(m, i) for m in others] for i in range(len(lists))]
    carried, routing = [], []

    def add_terms(step, opens, cut, outs, after):
        arrays = [a for m, i in step for a in (hidden[i][m], hidden[i][m ^ 1])]
        terms = [(m, lists[i]) for m, i in step]
        with jax.named_scope("down"):
            return call(
                functools.partial(down_kernel, rows, n_dp, flips, terms, opens, cut),
                outs,
                [*arrays, *(info, in_vmem(down), shrink2), *carried, *routing, *after],
                room=(6 << 20) + 4 * all_rows * (4 * cols + 2 * packed_rows + 4 * part),
            )

    for s, step in enumerate(steps[:-1]):
        if s == 1:
            between_cores(hidden[-1], others, carried)
        outs = list(sums)
        if s == 0:
            outs += [shape((all_rows, ranks), F32)] + ([spreads] if flips else [])
        carried = add_terms(step, s == 0, None, outs, [])
        if s == 0:
            carried, routing = carried[:2], carried[2:]
    if len(steps) == 2:
        between_cores(hidden[-1], others, carried)

    some = width // PARTS
    arrived, after = [], [expand2]
    for cut in range(PARTS):
        outs = [shape((half_rows, some), F32), shape((half_rows, some))]
        ready = shape((all_rows, ranks))
        keep, send, *more = add_terms(
            steps[-1], False, cut, outs + ([ready] if cut == 0 else []), after
        )
        after = after + more
        terms, left = [keep, over(send, "dp", 1)], n_x
        for b in x_bits[::-1]:
            left //= 2
            dims = (n_z * left * rows, some)
            kept = call(
                functools.partial(add_and_deal, left * rows, 2, 1),
                [shape(dims, F32), shape(dims)],
                terms,
                room=(2 << 20) + 3 * size_of(terms[0]),
            )
            terms = [kept[0], over(kept[1], "dp", b)]
        arrived += terms
    kept = call(
        functools.partial(add_and_deal, rows, 2, PARTS),
        [shape((rows, width), F32)] + [shape((rows, width))] * (n_z - 1),
        arrived,
        room=(2 << 20) + 6 * size_of(arrived[0]),
    )
    back = [over(kept[k], "expert", k) for k in range(n_z - 1, 0, -1)]
    with jax.named_scope("finish"):
        return call(
            functools.partial(finish, cols),
            shape((rows, width)),
            [kept[0], *back],
        )


def solution(mesh):
    rows = ("group", "expert", "dp")
    in_specs = (
        P(rows, None),
        P(rows, None),
        P(rows, None),
        P(rows),
        P("expert", None, "dp"),
        P("expert", None, "dp"),
        P("expert", None, "dp"),
        P("expert", "dp", None, None),
        P("expert", "dp", None, None),
        P(),
        P(),
    )
    return jax.shard_map(
        shards, mesh=mesh, in_specs=in_specs, out_specs=P(rows, None), check_vma=False
    )
```

```python
import functools

import jax
import jax.numpy as jnp
from jax import lax
from jax.experimental import pallas as pl
from jax.experimental.pallas import tpu as pltpu
from jax.sharding import PartitionSpec as P

TOP = 8
EXPERTS = 16
SLOTS = 2
CAP = 3
LANES = 128
PIECES = 3
PARTS = 2
BF = jnp.bfloat16
F32 = jnp.float32

VM = pl.BlockSpec(memory_space=pltpu.VMEM)
HB = pl.BlockSpec(memory_space=pltpu.HBM)


def in_vmem(x):
    return pltpu.with_memory_space_constraint(x, pltpu.VMEM)


def in_hbm(x):
    return pltpu.with_memory_space_constraint(x, pltpu.HBM)


def shape(dims, dtype=BF):
    return jax.ShapeDtypeStruct(tuple(dims), dtype)


def size_of(*arrays):
    total = 0
    for a in arrays:
        n = jnp.dtype(a.dtype).itemsize
        for s in a.shape[:-1]:
            n *= s
        total += n * (-(-a.shape[-1] // LANES) * LANES)
    return total


def call(body, out_shape, operands, specs=None, room=2 << 20, scratch=(), in_place=False):
    specs = specs or [VM] * len(operands)
    held = [a for a, s in zip(operands, specs) if s is VM and size_of(a) < 1 << 20]
    limit = room + size_of(*held, *jax.tree.leaves(out_shape))
    return pl.pallas_call(
        body,
        out_shape=out_shape,
        in_specs=specs,
        out_specs=jax.tree.map(lambda _: VM, out_shape),
        scratch_shapes=scratch,
        input_output_aliases={0: 0} if in_place else {},
        cost_estimate=pl.CostEstimate(flops=0, bytes_accessed=0, transcendentals=0),
        compiler_params=pltpu.CompilerParams(vmem_limit_bytes=limit),
    )(*operands)


def prepare(*refs):
    ins, y, held, sems = refs[:6], refs[9], refs[10:16], refs[16]
    copies = [pltpu.make_async_copy(s, d, sems.at[i]) for i, (s, d) in enumerate(zip(ins, held))]
    for c in copies:
        c.start()
    for c in copies:
        c.wait()
    ten, tok, ids, rw, owner, slot = held
    rows, width = tok.shape
    y[:, :width] = tok[...]
    lane = lax.broadcasted_iota(jnp.int32, (rows, LANES), 1)
    expert, piece = lane & (EXPERTS - 1), lane >> (EXPERTS.bit_length() - 1)
    w = jnp.zeros((rows, LANES), F32)
    routed = jnp.zeros((rows, LANES), F32)
    for k in range(TOP):
        same = ids[:, k : k + 1] == expert
        w += jnp.where(same, rw[:, k : k + 1], 0.0)
        routed += jnp.where(same, 1.0, 0.0)
    places = [routed[:1]]
    for r in range(1, rows):
        places.append(places[-1] + routed[r : r + 1])
    place = jnp.concatenate(places, axis=0) * routed
    high = w.astype(BF).astype(F32)
    mid = (w - high).astype(BF).astype(F32)
    low = w - high - mid
    pages = [
        owner[pl.ds(ten[r], 1), :] * SLOTS + slot[pl.ds(ten[r], 1), :] for r in range(rows)
    ]
    slots = jnp.concatenate(pages, axis=0).astype(F32)
    block = jnp.concatenate([slots] * (LANES // EXPERTS), axis=1)
    for i, value in enumerate((high, mid, low, place)):
        block = jnp.where(piece == i, value, block)
    y[:, width:] = block.astype(BF)


def join_blocks(count, *refs):
    parts = [r[...].astype(F32) for r in refs[:count]]
    refs[-1][...] = jnp.concatenate(parts, axis=0).astype(BF)


def relay(x, *refs):
    pass


def column(meta, lane, wanted):
    return jnp.sum(jnp.where(lane == wanted, meta, 0.0), axis=1, keepdims=True)


def picks(meta, lane, expert, each, flip):
    rows = meta.shape[0]
    place = column(meta, lane, PIECES * EXPERTS + expert).astype(jnp.int32)
    block = lax.broadcasted_iota(jnp.int32, (rows, 1), 0) >> (each.bit_length() - 1)
    target = jnp.where(place > 0, (block ^ flip) * CAP + place - 1, -1)
    slots = rows // each * CAP
    spot = lax.broadcasted_iota(jnp.int32, (rows, slots), 1)
    return jnp.where(spot == target, 1.0, 0.0).astype(BF)


def gather_rows(places, *refs):
    blocks, xs, info = refs[: len(places)], refs[-2], refs[-1]
    size, width = blocks[0].shape[0], xs.shape[1]
    in_order = [blocks[places.index(i)] for i in range(len(places))]
    for i in range(0, len(places), 2):
        pair = [r[...].astype(F32) for r in in_order[i : i + 2]]
        both = jnp.concatenate(pair, axis=0).astype(BF)
        xs[i * size : (i + 2) * size] = both[:, :width]
        info[i * size : (i + 2) * size] = both[:, width:]


def up_kernel(picked, each, *refs):
    xs, info, gate, up, h, *packed = refs
    experts, width = gate.shape[0], gate.shape[1]
    first = lax.axis_index("expert") * experts
    meta = info[...].astype(F32)
    lane = lax.broadcasted_iota(jnp.int32, meta.shape, 1)
    weight = jnp.where(lane < PIECES * EXPERTS, meta, 0.0)
    step = 256
    for i, e in enumerate(picked):
        w = column(weight, lane & (EXPERTS - 1), first + e)
        a = b = 0.0
        for k in range(0, width, step):
            x = xs[:, k : k + step]
            a += jnp.dot(x, gate[e, k : k + step], preferred_element_type=F32)
            b += jnp.dot(x, up[e, k : k + step], preferred_element_type=F32)
        hidden = (a * jax.nn.sigmoid(a) * b * w).astype(BF)
        h[i] = hidden
        if not packed:
            continue
        packed[0][i] = lax.dot_general(
            picks(meta, lane, first + e, each, 0),
            hidden,
            (((0,), (0,)), ((), ())),
            preferred_element_type=F32,
        ).astype(BF)


def columns(ref, spot, size):
    if size % LANES == 0:
        return ref[:, pl.ds(pl.multiple_of(spot * size, size), size)]
    picked = ref[:, :size]
    for c in range(1, ref.shape[1] // size):
        picked = jnp.where(spot == c, ref[:, c * size : (c + 1) * size], picked)
    return picked


def down_kernel(each, n, flips, terms, opens, cut, *refs):
    count = sum(len(arrays) for _, _, arrays in terms)
    pairs, refs = refs[:count], refs[count:]
    (info, down, shrink), refs = refs[:3], refs[3:]
    base = small = spreads = here_ref = None
    if not opens:
        base, small, here_ref = refs[0][...], refs[1][...], refs[2]
        refs = refs[3:]
        if flips:
            spreads, refs = refs[0], refs[1:]
    me = lax.axis_index("dp")
    odd = lax.rem(me, 2) == 1
    experts = down.shape[0]
    part = pairs[0].shape[2]
    rows, ranks = info.shape[0], shrink.shape[0]
    half, per = rows // 2, ranks // experts
    cols = down.shape[2]
    across = slice(0, cols)
    if cut is not None:
        across = slice(cut * (cols // PARTS), (cut + 1) * (cols // PARTS))
        base = base[:, across]
    first = lax.axis_index("expert") * experts
    meta = info[...].astype(F32)
    lane16 = lax.broadcasted_iota(jnp.int32, meta.shape, 1)
    lane = lax.broadcasted_iota(jnp.int32, (rows, ranks), 1)

    def spread(e, m):
        flip = (m & 1) * (half // each) + (m >> 1)
        return picks(meta, lane16, first + e, each, flip)

    def turned(m):
        flip = (m & 1) * (half // each) + (m >> 1)
        there = lax.broadcasted_iota(jnp.int32, (rows, rows), 0) ^ (flip * each)
        return jnp.where(lax.broadcasted_iota(jnp.int32, (rows, rows), 1) == there, 1.0, 0.0).astype(BF)

    def ordered(ref, i, e, m):
        if m == 0:
            return ref[i]
        if ref.shape[1] == rows and m == 1:
            return jnp.concatenate([ref[i, half:], ref[i, :half]], axis=0)
        if ref.shape[1] == rows:
            return jnp.dot(turned(m), ref[i], preferred_element_type=F32).astype(BF)
        known = spreads is not None and m in flips
        one_hot = spreads[flips.index(m) * experts + e] if known else spread(e, m)
        return jnp.dot(one_hot, ref[i], preferred_element_type=F32).astype(BF)

    for m, picked, arrays in terms:
        got, pairs = pairs[: len(arrays)], pairs[len(arrays) :]
        for i, e in enumerate(picked):
            x = [ordered(r, i, e, m ^ o) for r, o in zip(got, arrays)]
            spots = [me ^ m ^ o for o in arrays]
            if len(x) == 2:
                x = [jnp.where(odd, x[1], x[0]), jnp.where(odd, x[0], x[1])]
                low = (me ^ m) // 2 * 2
                spots = [low, low + 1]
                if part % LANES == 0:
                    x, spots = [jnp.concatenate(x, axis=1)], [low // 2]
            for piece, spot in zip(x, spots):
                size = piece.shape[1]
                at = pl.ds(pl.multiple_of(spot * size, size), size)
                term = jnp.dot(piece, down[e, at, across], preferred_element_type=F32)
                base = term if base is None else base + term
                if cut:
                    continue
                term = lax.dot_general(
                    piece,
                    columns(shrink, spot, size),
                    (((1,), (1,)), ((), ())),
                    preferred_element_type=F32,
                )
                inside = (lane >= e * per) & (lane < (e + 1) * per)
                term = jnp.where(inside, term, 0.0)
                small = term if small is None else small + term
    if opens:
        refs[0][...] = base
        refs[1][...] = small
        rank = per // SLOTS
        away = jnp.full((rows, ranks), -1.0, F32)
        for e in range(experts):
            value = column(meta, lane16, (PIECES + 1) * EXPERTS + first + e)
            for s in range(SLOTS):
                low = e * per + s * rank
                inside = (lane >= low) & (lane < low + rank)
                away = jnp.where(inside, value - (me * SLOTS + s).astype(F32), away)
        refs[2][...] = jnp.where(away == 0.0, 1.0, 0.0)
        for f, m in enumerate(flips):
            for e in range(experts):
                refs[3][f * experts + e] = spread(e, m)
        return
    if cut is None:
        refs[0][...] = base
        refs[1][...] = small
        return
    if cut == 0:
        expand, keep, send, ready = refs
        small = (small * here_ref[...]).astype(BF)
        ready[...] = small
    else:
        expand, ready, keep, send = refs
        small = ready[...]
    size = cols // PARTS
    for c in range(n):
        here = slice(c * size, (c + 1) * size)
        there = slice(c * cols + across.start, c * cols + across.stop)
        out = jnp.dot(small, expand[:, there], preferred_element_type=F32)
        out += jnp.where(me == c, base, 0.0)
        keep[:, here] = out[:half]
        send[:, here] = out[half:].astype(BF)


def add_and_deal(size, count, sets, *refs):
    ins, outs = refs[: count * sets], refs[count * sets :]
    width = ins[0].shape[1]
    for s in range(sets):
        total = ins[s * count][...]
        for r in ins[s * count + 1 : (s + 1) * count]:
            total += r[...].astype(F32)
        parts = [total[r : r + size] for r in range(0, total.shape[0], size)]
        for i, o in enumerate(outs):
            dealt = jnp.concatenate(parts[i :: len(outs)], axis=0)
            o[:, s * width : (s + 1) * width] = dealt.astype(o.dtype)


def finish(cols, *refs):
    total = refs[0][...]
    for r in refs[1:-1]:
        total += r[...].astype(F32)
    size, n = cols // PARTS, total.shape[1] // cols
    for p in range(PARTS):
        for c in range(n):
            at = (p * n + c) * size
            to = c * cols + p * size
            refs[-1][:, to : to + size] = total[:, at : at + size].astype(BF)


def shards(tokens, expert_ids, route_weight, tenant_ids, gate, up, down, shrink, expand, owner, slot):
    n_z, n_dp = lax.axis_size("expert"), lax.axis_size("dp")
    n_x = n_dp // 2
    rows, width = tokens.shape
    experts, _, part = gate.shape
    wide = width + LANES
    block = rows * n_x
    half_rows = block * n_z
    all_rows = 2 * half_rows
    x_bits = [b for b in (2, 4, 8, 16, 32, 64) if b < n_dp]

    def over(x, axis, m):
        return lax.ppermute(x, axis, [(i, i ^ m) for i in range(lax.axis_size(axis))])

    inputs = (tenant_ids, tokens, expert_ids, route_weight, owner, slot)
    weights = [in_hbm(a) for a in (gate, up, down)]
    with jax.named_scope("prepare"):
        y = call(
            prepare,
            shape((rows, wide)),
            [*[in_hbm(a) for a in inputs], *weights],
            [HB] * (len(inputs) + 3),
            scratch=[
                *[(pltpu.VMEM if i else pltpu.SMEM)(a.shape, a.dtype) for i, a in enumerate(inputs)],
                pltpu.SemaphoreType.DMA((len(inputs),)),
            ],
        )

    blocks = [y]
    for b in x_bits:
        blocks = blocks + [over(a, "dp", b) for a in blocks]
    with jax.named_scope("join"):
        lead = call(
            functools.partial(join_blocks, n_x),
            shape((block, wide)),
            (*blocks, *weights),
            [VM] * n_x + [HB] * 3,
            room=(2 << 20) + 4 * block * wide,
        )
    along_z = {k: over(lead, "expert", k) if k else lead for k in range(n_z)}
    places = [0, *range(n_z - 1, 0, -1)]
    places += [k + n_z for k in places]
    gathered = [along_z[k] for k in places[:n_z]]
    gathered += [over(a, "dp", 1) for a in gathered]

    lists = [list(range(experts))]
    if experts > 1:
        lists = [lists[0][: experts // 2], lists[0][experts // 2 :]]
    packed_rows = all_rows // rows * CAP
    with jax.named_scope("gather"):
        xs, info = call(
            functools.partial(gather_rows, places),
            [shape((all_rows, width)), shape((all_rows, LANES))],
            gathered,
        )
    hidden = []
    for picked in lists:
        with jax.named_scope("up"):
            outs = [shape((len(picked), all_rows, part))]
            if picked is lists[-1]:
                outs.append(shape((len(picked), packed_rows, part)))
            h, *packed = call(
                functools.partial(up_kernel, picked, rows),
                outs,
                (xs, info, in_vmem(gate), in_vmem(up)),
                room=(4 << 20) + 4 * all_rows * (packed_rows + 4 * part + 8 * LANES),
            )
        hidden.append({0: h, "sent": packed[0] if packed else h})
    for got in hidden:
        moved = {0: got["sent"]}
        for b in x_bits:
            moved.update({m | b: over(a, "dp", b) for m, a in moved.items()})
        got.update({m: a for m, a in moved.items() if m})

    def between_cores(got, pairs, behind=()):
        for m in pairs:
            x = got[m] if m else got["sent"]
            if behind:
                x = got[m] = call(relay, shape(x.shape), (x, *behind), in_place=True)
            got[m ^ 1] = over(x, "dp", 1)

    others = list(range(2, n_dp, 2))
    for got in hidden:
        between_cores(got, [0] if got is hidden[-1] else [0, *others])

    shrink2 = shrink.reshape(-1, shrink.shape[-1])
    expand2 = expand.reshape(-1, expand.shape[-1])
    cols = down.shape[2]
    ranks = shrink2.shape[0]
    sums = [shape((all_rows, cols), F32), shape((all_rows, ranks), F32)]
    spreads = shape(((n_dp - 2) * experts, all_rows, packed_rows))
    flips = list(range(2, n_dp)) if size_of(spreads) < 1 << 20 else []
    both, last = (0, 1), len(lists) - 1
    steps = [[(0, i, both) for i in range(len(lists))]]
    steps[0] += [(m, i, (0,)) for i in range(last) for m in others]
    steps += [[(m, i, (int(i < last),)) for i in range(len(lists)) for m in others]]
    steps += [[(m, last, (1,)) for m in others]]
    carried, routing = [], []

    def add_terms(step, opens, cut, outs, after):
        arrays = [hidden[i][m ^ o] for m, i, cores in step for o in cores]
        terms = [(m, lists[i], cores) for m, i, cores in step]
        with jax.named_scope("down"):
            return call(
                functools.partial(down_kernel, rows, n_dp, flips, terms, opens, cut),
                outs,
                [*arrays, *(info, in_vmem(down), shrink2), *carried, *routing, *after],
                room=(6 << 20) + 4 * all_rows * (4 * cols + 2 * packed_rows + 4 * part),
            )

    for s, step in enumerate(steps[:-1]):
        if s == 1:
            between_cores(hidden[-1], others, carried)
        outs = list(sums)
        if s == 0:
            outs += [shape((all_rows, ranks), F32)] + ([spreads] if flips else [])
        carried = add_terms(step, s == 0, None, outs, [])
        if s == 0:
            carried, routing = carried[:2], carried[2:]

    some = width // PARTS
    arrived, after = [], [expand2]
    for cut in range(PARTS):
        outs = [shape((half_rows, some), F32), shape((half_rows, some))]
        ready = shape((all_rows, ranks))
        keep, send, *more = add_terms(
            steps[-1], False, cut, outs + ([ready] if cut == 0 else []), after
        )
        after = after + more
        terms, left = [keep, over(send, "dp", 1)], n_x
        for b in x_bits[::-1]:
            left //= 2
            dims = (n_z * left * rows, some)
            kept = call(
                functools.partial(add_and_deal, left * rows, 2, 1),
                [shape(dims, F32), shape(dims)],
                terms,
                room=(2 << 20) + 3 * size_of(terms[0]),
            )
            terms = [kept[0], over(kept[1], "dp", b)]
        arrived += terms
    kept = call(
        functools.partial(add_and_deal, rows, 2, PARTS),
        [shape((rows, width), F32)] + [shape((rows, width))] * (n_z - 1),
        arrived,
        room=(2 << 20) + 6 * size_of(arrived[0]),
    )
    back = [over(kept[k], "expert", k) for k in range(n_z - 1, 0, -1)]
    with jax.named_scope("finish"):
        return call(
            functools.partial(finish, cols),
            shape((rows, width)),
            [kept[0], *back],
        )


def solution(mesh):
    rows = ("group", "expert", "dp")
    in_specs = (
        P(rows, None),
        P(rows, None),
        P(rows, None),
        P(rows),
        P("expert", None, "dp"),
        P("expert", None, "dp"),
        P("expert", None, "dp"),
        P("expert", "dp", None, None),
        P("expert", "dp", None, None),
        P(),
        P(),
    )
    return jax.shard_map(
        shards, mesh=mesh, in_specs=in_specs, out_specs=P(rows, None), check_vma=False
    )
```

```python
import functools

import jax
import jax.numpy as jnp
from jax import lax
from jax.experimental import pallas as pl
from jax.experimental.pallas import tpu as pltpu
from jax.sharding import PartitionSpec as P

TOP = 8
EXPERTS = 16
SLOTS = 2
CAP = 3
LANES = 128
PIECES = 3
PARTS = 2
BF = jnp.bfloat16
F32 = jnp.float32

VM = pl.BlockSpec(memory_space=pltpu.VMEM)
HB = pl.BlockSpec(memory_space=pltpu.HBM)


def in_vmem(x):
    return pltpu.with_memory_space_constraint(x, pltpu.VMEM)


def in_hbm(x):
    return pltpu.with_memory_space_constraint(x, pltpu.HBM)


def shape(dims, dtype=BF):
    return jax.ShapeDtypeStruct(tuple(dims), dtype)


def size_of(*arrays):
    total = 0
    for a in arrays:
        n = jnp.dtype(a.dtype).itemsize
        for s in a.shape[:-1]:
            n *= s
        total += n * (-(-a.shape[-1] // LANES) * LANES)
    return total


def call(body, out_shape, operands, specs=None, room=2 << 20, scratch=(), in_place=False):
    specs = specs or [VM] * len(operands)
    held = [a for a, s in zip(operands, specs) if s is VM and size_of(a) < 1 << 20]
    limit = room + size_of(*held, *jax.tree.leaves(out_shape))
    return pl.pallas_call(
        body,
        out_shape=out_shape,
        in_specs=specs,
        out_specs=jax.tree.map(lambda _: VM, out_shape),
        scratch_shapes=scratch,
        input_output_aliases={0: 0} if in_place else {},
        cost_estimate=pl.CostEstimate(flops=0, bytes_accessed=0, transcendentals=0),
        compiler_params=pltpu.CompilerParams(vmem_limit_bytes=limit),
    )(*operands)


def prepare(*refs):
    ins, y, held, sems = refs[:6], refs[9], refs[10:16], refs[16]
    copies = [pltpu.make_async_copy(s, d, sems.at[i]) for i, (s, d) in enumerate(zip(ins, held))]
    for c in copies:
        c.start()
    for c in copies:
        c.wait()
    ten, tok, ids, rw, owner, slot = held
    rows, width = tok.shape
    y[:, :width] = tok[...]
    lane = lax.broadcasted_iota(jnp.int32, (rows, LANES), 1)
    expert, piece = lane & (EXPERTS - 1), lane >> (EXPERTS.bit_length() - 1)
    w = jnp.zeros((rows, LANES), F32)
    routed = jnp.zeros((rows, LANES), F32)
    for k in range(TOP):
        same = ids[:, k : k + 1] == expert
        w += jnp.where(same, rw[:, k : k + 1], 0.0)
        routed += jnp.where(same, 1.0, 0.0)
    places = [routed[:1]]
    for r in range(1, rows):
        places.append(places[-1] + routed[r : r + 1])
    place = jnp.concatenate(places, axis=0) * routed
    high = w.astype(BF).astype(F32)
    mid = (w - high).astype(BF).astype(F32)
    low = w - high - mid
    pages = [
        owner[pl.ds(ten[r], 1), :] * SLOTS + slot[pl.ds(ten[r], 1), :] for r in range(rows)
    ]
    slots = jnp.concatenate(pages, axis=0).astype(F32)
    block = jnp.concatenate([slots] * (LANES // EXPERTS), axis=1)
    for i, value in enumerate((high, mid, low, place)):
        block = jnp.where(piece == i, value, block)
    y[:, width:] = block.astype(BF)


def join_blocks(count, *refs):
    parts = [r[...].astype(F32) for r in refs[:count]]
    refs[-1][...] = jnp.concatenate(parts, axis=0).astype(BF)


def relay(x, *refs):
    refs[-1][...] = x[...]


def column(meta, lane, wanted):
    return jnp.sum(jnp.where(lane == wanted, meta, 0.0), axis=1, keepdims=True)


def picks(meta, lane, expert, each, flip):
    rows = meta.shape[0]
    place = column(meta, lane, PIECES * EXPERTS + expert).astype(jnp.int32)
    block = lax.broadcasted_iota(jnp.int32, (rows, 1), 0) >> (each.bit_length() - 1)
    target = jnp.where(place > 0, (block ^ flip) * CAP + place - 1, -1)
    slots = rows // each * CAP
    spot = lax.broadcasted_iota(jnp.int32, (rows, slots), 1)
    return jnp.where(spot == target, 1.0, 0.0).astype(BF)


def gather_rows(places, *refs):
    blocks, xs, info = refs[: len(places)], refs[-2], refs[-1]
    size, width = blocks[0].shape[0], xs.shape[1]
    in_order = [blocks[places.index(i)] for i in range(len(places))]
    for i in range(0, len(places), 2):
        pair = [r[...].astype(F32) for r in in_order[i : i + 2]]
        both = jnp.concatenate(pair, axis=0).astype(BF)
        xs[i * size : (i + 2) * size] = both[:, :width]
        info[i * size : (i + 2) * size] = both[:, width:]


def up_kernel(picked, each, *refs):
    xs, info, gate, up, h, *packed = refs
    experts, width = gate.shape[0], gate.shape[1]
    first = lax.axis_index("expert") * experts
    meta = info[...].astype(F32)
    lane = lax.broadcasted_iota(jnp.int32, meta.shape, 1)
    weight = jnp.where(lane < PIECES * EXPERTS, meta, 0.0)
    step = 256
    for i, e in enumerate(picked):
        w = column(weight, lane & (EXPERTS - 1), first + e)
        a = b = 0.0
        for k in range(0, width, step):
            x = xs[:, k : k + step]
            a += jnp.dot(x, gate[e, k : k + step], preferred_element_type=F32)
            b += jnp.dot(x, up[e, k : k + step], preferred_element_type=F32)
        hidden = (a * jax.nn.sigmoid(a) * b * w).astype(BF)
        h[i] = hidden
        if not packed:
            continue
        packed[0][i] = lax.dot_general(
            picks(meta, lane, first + e, each, 0),
            hidden,
            (((0,), (0,)), ((), ())),
            preferred_element_type=F32,
        ).astype(BF)


def columns(ref, spot, size):
    if size % LANES == 0:
        return ref[:, pl.ds(pl.multiple_of(spot * size, size), size)]
    picked = ref[:, :size]
    for c in range(1, ref.shape[1] // size):
        picked = jnp.where(spot == c, ref[:, c * size : (c + 1) * size], picked)
    return picked


def down_kernel(each, n, flips, terms, opens, cut, *refs):
    count = sum(len(arrays) for _, _, arrays in terms)
    pairs, refs = refs[:count], refs[count:]
    (info, down, shrink), refs = refs[:3], refs[3:]
    base = small = spreads = here_ref = None
    if not opens:
        base, small, here_ref = refs[0][...], refs[1][...], refs[2]
        refs = refs[3:]
        if flips:
            spreads, refs = refs[0], refs[1:]
    me = lax.axis_index("dp")
    odd = lax.rem(me, 2) == 1
    experts = down.shape[0]
    part = pairs[0].shape[2]
    rows, ranks = info.shape[0], shrink.shape[0]
    half, per = rows // 2, ranks // experts
    cols = down.shape[2]
    across = slice(0, cols)
    if cut is not None:
        across = slice(cut * (cols // PARTS), (cut + 1) * (cols // PARTS))
        base = base[:, across]
    first = lax.axis_index("expert") * experts
    meta = info[...].astype(F32)
    lane16 = lax.broadcasted_iota(jnp.int32, meta.shape, 1)
    lane = lax.broadcasted_iota(jnp.int32, (rows, ranks), 1)

    def spread(e, m):
        flip = (m & 1) * (half // each) + (m >> 1)
        return picks(meta, lane16, first + e, each, flip)

    def turned(m):
        flip = (m & 1) * (half // each) + (m >> 1)
        there = lax.broadcasted_iota(jnp.int32, (rows, rows), 0) ^ (flip * each)
        return jnp.where(lax.broadcasted_iota(jnp.int32, (rows, rows), 1) == there, 1.0, 0.0).astype(BF)

    def ordered(ref, i, e, m):
        if m == 0:
            return ref[i]
        if ref.shape[1] == rows and m == 1:
            return jnp.concatenate([ref[i, half:], ref[i, :half]], axis=0)
        if ref.shape[1] == rows:
            return jnp.dot(turned(m), ref[i], preferred_element_type=F32).astype(BF)
        known = spreads is not None and m in flips
        one_hot = spreads[flips.index(m) * experts + e] if known else spread(e, m)
        return jnp.dot(one_hot, ref[i], preferred_element_type=F32).astype(BF)

    for m, picked, arrays in terms:
        got, pairs = pairs[: len(arrays)], pairs[len(arrays) :]
        for i, e in enumerate(picked):
            x = [ordered(r, i, e, m ^ o) for r, o in zip(got, arrays)]
            spots = [me ^ m ^ o for o in arrays]
            if len(x) == 2:
                x = [jnp.where(odd, x[1], x[0]), jnp.where(odd, x[0], x[1])]
                low = (me ^ m) // 2 * 2
                spots = [low, low + 1]
                if part % LANES == 0:
                    x, spots = [jnp.concatenate(x, axis=1)], [low // 2]
            for piece, spot in zip(x, spots):
                size = piece.shape[1]
                at = pl.ds(pl.multiple_of(spot * size, size), size)
                term = jnp.dot(piece, down[e, at, across], preferred_element_type=F32)
                base = term if base is None else base + term
                if cut:
                    continue
                term = lax.dot_general(
                    piece,
                    columns(shrink, spot, size),
                    (((1,), (1,)), ((), ())),
                    preferred_element_type=F32,
                )
                inside = (lane >= e * per) & (lane < (e + 1) * per)
                term = jnp.where(inside, term, 0.0)
                small = term if small is None else small + term
    if opens:
        refs[0][...] = base
        refs[1][...] = small
        rank = per // SLOTS
        away = jnp.full((rows, ranks), -1.0, F32)
        for e in range(experts):
            value = column(meta, lane16, (PIECES + 1) * EXPERTS + first + e)
            for s in range(SLOTS):
                low = e * per + s * rank
                inside = (lane >= low) & (lane < low + rank)
                away = jnp.where(inside, value - (me * SLOTS + s).astype(F32), away)
        refs[2][...] = jnp.where(away == 0.0, 1.0, 0.0)
        for f, m in enumerate(flips):
            for e in range(experts):
                refs[3][f * experts + e] = spread(e, m)
        return
    if cut is None:
        refs[0][...] = base
        refs[1][...] = small
        return
    if cut == 0:
        expand, keep, send, ready = refs
        small = (small * here_ref[...]).astype(BF)
        ready[...] = small
    else:
        expand, ready, keep, send = refs
        small = ready[...]
    size = cols // PARTS
    for c in range(n):
        here = slice(c * size, (c + 1) * size)
        there = slice(c * cols + across.start, c * cols + across.stop)
        out = jnp.dot(small, expand[:, there], preferred_element_type=F32)
        out += jnp.where(me == c, base, 0.0)
        keep[:, here] = out[:half]
        send[:, here] = out[half:].astype(BF)


def add_and_deal(size, count, sets, *refs):
    ins, outs = refs[: count * sets], refs[count * sets :]
    width = ins[0].shape[1]
    for s in range(sets):
        total = ins[s * count][...]
        for r in ins[s * count + 1 : (s + 1) * count]:
            total += r[...].astype(F32)
        parts = [total[r : r + size] for r in range(0, total.shape[0], size)]
        for i, o in enumerate(outs):
            dealt = jnp.concatenate(parts[i :: len(outs)], axis=0)
            o[:, s * width : (s + 1) * width] = dealt.astype(o.dtype)


def finish(cols, *refs):
    total = refs[0][...]
    for r in refs[1:-1]:
        total += r[...].astype(F32)
    size, n = cols // PARTS, total.shape[1] // cols
    for p in range(PARTS):
        for c in range(n):
            at = (p * n + c) * size
            to = c * cols + p * size
            refs[-1][:, to : to + size] = total[:, at : at + size].astype(BF)


def shards(tokens, expert_ids, route_weight, tenant_ids, gate, up, down, shrink, expand, owner, slot):
    n_z, n_dp = lax.axis_size("expert"), lax.axis_size("dp")
    n_x = n_dp // 2
    rows, width = tokens.shape
    experts, _, part = gate.shape
    wide = width + LANES
    block = rows * n_x
    half_rows = block * n_z
    all_rows = 2 * half_rows
    x_bits = [b for b in (2, 4, 8, 16, 32, 64) if b < n_dp]

    def over(x, axis, m):
        return lax.ppermute(x, axis, [(i, i ^ m) for i in range(lax.axis_size(axis))])

    inputs = (tenant_ids, tokens, expert_ids, route_weight, owner, slot)
    weights = [in_hbm(a) for a in (gate, up, down)]
    with jax.named_scope("prepare"):
        y = call(
            prepare,
            shape((rows, wide)),
            [*[in_hbm(a) for a in inputs], *weights],
            [HB] * (len(inputs) + 3),
            scratch=[
                *[(pltpu.VMEM if i else pltpu.SMEM)(a.shape, a.dtype) for i, a in enumerate(inputs)],
                pltpu.SemaphoreType.DMA((len(inputs),)),
            ],
        )

    blocks = [y]
    for b in x_bits:
        blocks = blocks + [over(a, "dp", b) for a in blocks]
    with jax.named_scope("join"):
        lead = call(
            functools.partial(join_blocks, n_x),
            shape((block, wide)),
            (*blocks, *weights),
            [VM] * n_x + [HB] * 3,
            room=(2 << 20) + 4 * block * wide,
        )
    along_z = {k: over(lead, "expert", k) if k else lead for k in range(n_z)}
    places = [0, *range(n_z - 1, 0, -1)]
    places += [k + n_z for k in places]
    gathered = [along_z[k] for k in places[:n_z]]
    gathered += [over(a, "dp", 1) for a in gathered]

    lists = [list(range(experts))]
    if experts > 1:
        lists = [lists[0][: experts // 2], lists[0][experts // 2 :]]
    packed_rows = all_rows // rows * CAP
    with jax.named_scope("gather"):
        xs, info = call(
            functools.partial(gather_rows, places),
            [shape((all_rows, width)), shape((all_rows, LANES))],
            gathered,
        )
    hidden = []
    for picked in lists:
        with jax.named_scope("up"):
            outs = [shape((len(picked), all_rows, part))]
            if picked is lists[-1]:
                outs.append(shape((len(picked), packed_rows, part)))
            h, *packed = call(
                functools.partial(up_kernel, picked, rows),
                outs,
                (xs, info, in_vmem(gate), in_vmem(up)),
                room=(4 << 20) + 4 * all_rows * (packed_rows + 4 * part + 8 * LANES),
            )
        hidden.append({0: h, "sent": packed[0] if packed else h})
    for got in hidden:
        moved = {0: got["sent"]}
        for b in x_bits:
            moved.update({m | b: over(a, "dp", b) for m, a in moved.items()})
        got.update({m: a for m, a in moved.items() if m})

    def between_cores(got, pairs, behind=()):
        for m in pairs:
            x = got[m] if m else got["sent"]
            if behind:
                x = got[m] = call(relay, shape(x.shape), (x, *behind), in_place=True)
            got[m ^ 1] = over(x, "dp", 1)

    others = list(range(2, n_dp, 2))
    for got in hidden:
        between_cores(got, [0] if got is hidden[-1] else [0, *others])

    shrink2 = shrink.reshape(-1, shrink.shape[-1])
    expand2 = expand.reshape(-1, expand.shape[-1])
    cols = down.shape[2]
    ranks = shrink2.shape[0]
    sums = [shape((all_rows, cols), F32), shape((all_rows, ranks), F32)]
    spreads = shape(((n_dp - 2) * experts, all_rows, packed_rows))
    flips = list(range(2, n_dp)) if size_of(spreads) < 1 << 20 else []
    both, last = (0, 1), len(lists) - 1
    steps = [[(0, i, both) for i in range(len(lists))]]
    steps[0] += [(m, i, (0,)) for i in range(last) for m in others]
    steps += [[(m, i, (int(i < last),)) for i in range(len(lists)) for m in others]]
    steps += [[(m, last, (1,)) for m in others]]
    carried, routing = [], []

    def add_terms(step, opens, cut, outs, after):
        arrays = [hidden[i][m ^ o] for m, i, cores in step for o in cores]
        terms = [(m, lists[i], cores) for m, i, cores in step]
        with jax.named_scope("down"):
            return call(
                functools.partial(down_kernel, rows, n_dp, flips, terms, opens, cut),
                outs,
                [*arrays, *(info, in_vmem(down), shrink2), *carried, *routing, *after],
                room=(6 << 20) + 4 * all_rows * (4 * cols + 2 * packed_rows + 4 * part),
            )

    for s, step in enumerate(steps[:-1]):
        if s == 1:
            between_cores(hidden[-1], others, carried)
        outs = list(sums)
        if s == 0:
            outs += [shape((all_rows, ranks), F32)] + ([spreads] if flips else [])
        carried = add_terms(step, s == 0, None, outs, [])
        if s == 0:
            carried, routing = carried[:2], carried[2:]

    some = width // PARTS
    arrived, after = [], [expand2]
    for cut in range(PARTS):
        outs = [shape((half_rows, some), F32), shape((half_rows, some))]
        ready = shape((all_rows, ranks))
        keep, send, *more = add_terms(
            steps[-1], False, cut, outs + ([ready] if cut == 0 else []), after
        )
        after = after + more
        terms, left = [keep, over(send, "dp", 1)], n_x
        for b in x_bits[::-1]:
            left //= 2
            dims = (n_z * left * rows, some)
            kept = call(
                functools.partial(add_and_deal, left * rows, 2, 1),
                [shape(dims, F32), shape(dims)],
                terms,
                room=(2 << 20) + 3 * size_of(terms[0]),
            )
            terms = [kept[0], over(kept[1], "dp", b)]
        arrived += terms
    kept = call(
        functools.partial(add_and_deal, rows, 2, PARTS),
        [shape((rows, width), F32)] + [shape((rows, width))] * (n_z - 1),
        arrived,
        room=(2 << 20) + 6 * size_of(arrived[0]),
    )
    back = [over(kept[k], "expert", k) for k in range(n_z - 1, 0, -1)]
    with jax.named_scope("finish"):
        return call(
            functools.partial(finish, cols),
            shape((rows, width)),
            [kept[0], *back],
        )


def solution(mesh):
    rows = ("group", "expert", "dp")
    in_specs = (
        P(rows, None),
        P(rows, None),
        P(rows, None),
        P(rows),
        P("expert", None, "dp"),
        P("expert", None, "dp"),
        P("expert", None, "dp"),
        P("expert", "dp", None, None),
        P("expert", "dp", None, None),
        P(),
        P(),
    )
    return jax.shard_map(
        shards, mesh=mesh, in_specs=in_specs, out_specs=P(rows, None), check_vma=False
    )
```

```python
import functools

import jax
import jax.numpy as jnp
from jax import lax
from jax.experimental import pallas as pl
from jax.experimental.pallas import tpu as pltpu
from jax.sharding import PartitionSpec as P

TOP = 8
EXPERTS = 16
SLOTS = 2
CAP = 3
LANES = 128
PIECES = 3
PARTS = 2
BF = jnp.bfloat16
F32 = jnp.float32

VM = pl.BlockSpec(memory_space=pltpu.VMEM)
HB = pl.BlockSpec(memory_space=pltpu.HBM)


def in_vmem(x):
    return pltpu.with_memory_space_constraint(x, pltpu.VMEM)


def in_hbm(x):
    return pltpu.with_memory_space_constraint(x, pltpu.HBM)


def shape(dims, dtype=BF):
    return jax.ShapeDtypeStruct(tuple(dims), dtype)


def size_of(*arrays):
    total = 0
    for a in arrays:
        n = jnp.dtype(a.dtype).itemsize
        for s in a.shape[:-1]:
            n *= s
        total += n * (-(-a.shape[-1] // LANES) * LANES)
    return total


def call(body, out_shape, operands, specs=None, room=2 << 20, scratch=(), in_place=False):
    specs = specs or [VM] * len(operands)
    held = [a for a, s in zip(operands, specs) if s is VM and size_of(a) < 1 << 20]
    limit = room + size_of(*held, *jax.tree.leaves(out_shape))
    return pl.pallas_call(
        body,
        out_shape=out_shape,
        in_specs=specs,
        out_specs=jax.tree.map(lambda _: VM, out_shape),
        scratch_shapes=scratch,
        input_output_aliases={0: 0} if in_place else {},
        cost_estimate=pl.CostEstimate(flops=0, bytes_accessed=0, transcendentals=0),
        compiler_params=pltpu.CompilerParams(vmem_limit_bytes=limit),
    )(*operands)


def prepare(*refs):
    ins, y, held, sems = refs[:6], refs[9], refs[10:16], refs[16]
    copies = [pltpu.make_async_copy(s, d, sems.at[i]) for i, (s, d) in enumerate(zip(ins, held))]
    for c in copies:
        c.start()
    for c in copies:
        c.wait()
    ten, tok, ids, rw, owner, slot = held
    rows, width = tok.shape
    y[:, :width] = tok[...]
    lane = lax.broadcasted_iota(jnp.int32, (rows, LANES), 1)
    expert, piece = lane & (EXPERTS - 1), lane >> (EXPERTS.bit_length() - 1)
    w = jnp.zeros((rows, LANES), F32)
    routed = jnp.zeros((rows, LANES), F32)
    for k in range(TOP):
        same = ids[:, k : k + 1] == expert
        w += jnp.where(same, rw[:, k : k + 1], 0.0)
        routed += jnp.where(same, 1.0, 0.0)
    places = [routed[:1]]
    for r in range(1, rows):
        places.append(places[-1] + routed[r : r + 1])
    place = jnp.concatenate(places, axis=0) * routed
    high = w.astype(BF).astype(F32)
    mid = (w - high).astype(BF).astype(F32)
    low = w - high - mid
    pages = [
        owner[pl.ds(ten[r], 1), :] * SLOTS + slot[pl.ds(ten[r], 1), :] for r in range(rows)
    ]
    slots = jnp.concatenate(pages, axis=0).astype(F32)
    block = jnp.concatenate([slots] * (LANES // EXPERTS), axis=1)
    for i, value in enumerate((high, mid, low, place)):
        block = jnp.where(piece == i, value, block)
    y[:, width:] = block.astype(BF)


def join_blocks(count, *refs):
    parts = [r[...].astype(F32) for r in refs[:count]]
    refs[-1][...] = jnp.concatenate(parts, axis=0).astype(BF)


def relay(x, *refs):
    refs[-1][...] = x[...]


def column(meta, lane, wanted):
    return jnp.sum(jnp.where(lane == wanted, meta, 0.0), axis=1, keepdims=True)


def picks(meta, lane, expert, each, flip):
    rows = meta.shape[0]
    place = column(meta, lane, PIECES * EXPERTS + expert).astype(jnp.int32)
    block = lax.broadcasted_iota(jnp.int32, (rows, 1), 0) >> (each.bit_length() - 1)
    target = jnp.where(place > 0, (block ^ flip) * CAP + place - 1, -1)
    slots = rows // each * CAP
    spot = lax.broadcasted_iota(jnp.int32, (rows, slots), 1)
    return jnp.where(spot == target, 1.0, 0.0).astype(BF)


def gather_rows(places, *refs):
    blocks, xs, info = refs[: len(places)], refs[-2], refs[-1]
    size, width = blocks[0].shape[0], xs.shape[1]
    in_order = [blocks[places.index(i)] for i in range(len(places))]
    for i in range(0, len(places), 2):
        pair = [r[...].astype(F32) for r in in_order[i : i + 2]]
        both = jnp.concatenate(pair, axis=0).astype(BF)
        xs[i * size : (i + 2) * size] = both[:, :width]
        info[i * size : (i + 2) * size] = both[:, width:]


def up_kernel(picked, each, *refs):
    xs, info, gate, up, h, *packed = refs
    experts, width = gate.shape[0], gate.shape[1]
    first = lax.axis_index("expert") * experts
    meta = info[...].astype(F32)
    lane = lax.broadcasted_iota(jnp.int32, meta.shape, 1)
    weight = jnp.where(lane < PIECES * EXPERTS, meta, 0.0)
    step = 256
    for i, e in enumerate(picked):
        w = column(weight, lane & (EXPERTS - 1), first + e)
        a = b = 0.0
        for k in range(0, width, step):
            x = xs[:, k : k + step]
            a += jnp.dot(x, gate[e, k : k + step], preferred_element_type=F32)
            b += jnp.dot(x, up[e, k : k + step], preferred_element_type=F32)
        hidden = (a * jax.nn.sigmoid(a) * b * w).astype(BF)
        h[i] = hidden
        if not packed:
            continue
        packed[0][i] = lax.dot_general(
            picks(meta, lane, first + e, each, 0),
            hidden,
            (((0,), (0,)), ((), ())),
            preferred_element_type=F32,
        ).astype(BF)


def columns(ref, spot, size):
    if size % LANES == 0:
        return ref[:, pl.ds(pl.multiple_of(spot * size, size), size)]
    picked = ref[:, :size]
    for c in range(1, ref.shape[1] // size):
        picked = jnp.where(spot == c, ref[:, c * size : (c + 1) * size], picked)
    return picked


def down_kernel(each, n, flips, terms, opens, cut, *refs):
    count = sum(len(arrays) for _, _, arrays in terms)
    pairs, refs = refs[:count], refs[count:]
    (info, down, shrink), refs = refs[:3], refs[3:]
    base = small = spreads = here_ref = None
    if not opens:
        base, small, here_ref = refs[0][...], refs[1][...], refs[2]
        refs = refs[3:]
        if flips:
            spreads, refs = refs[0], refs[1:]
    me = lax.axis_index("dp")
    odd = lax.rem(me, 2) == 1
    experts = down.shape[0]
    part = pairs[0].shape[2]
    rows, ranks = info.shape[0], shrink.shape[0]
    half, per = rows // 2, ranks // experts
    cols = down.shape[2]
    across = slice(0, cols)
    if cut is not None:
        across = slice(cut * (cols // PARTS), (cut + 1) * (cols // PARTS))
        base = base[:, across]
    first = lax.axis_index("expert") * experts
    meta = info[...].astype(F32)
    lane16 = lax.broadcasted_iota(jnp.int32, meta.shape, 1)
    lane = lax.broadcasted_iota(jnp.int32, (rows, ranks), 1)

    def spread(e, m):
        flip = (m & 1) * (half // each) + (m >> 1)
        return picks(meta, lane16, first + e, each, flip)

    def turned(m):
        flip = (m & 1) * (half // each) + (m >> 1)
        there = lax.broadcasted_iota(jnp.int32, (rows, rows), 0) ^ (flip * each)
        return jnp.where(lax.broadcasted_iota(jnp.int32, (rows, rows), 1) == there, 1.0, 0.0).astype(BF)

    def ordered(ref, i, e, m):
        if m == 0:
            return ref[i]
        if ref.shape[1] == rows and m == 1:
            return jnp.concatenate([ref[i, half:], ref[i, :half]], axis=0)
        if ref.shape[1] == rows:
            return jnp.dot(turned(m), ref[i], preferred_element_type=F32).astype(BF)
        known = spreads is not None and m in flips
        one_hot = spreads[flips.index(m) * experts + e] if known else spread(e, m)
        return jnp.dot(one_hot, ref[i], preferred_element_type=F32).astype(BF)

    for m, picked, arrays in terms:
        got, pairs = pairs[: len(arrays)], pairs[len(arrays) :]
        for i, e in enumerate(picked):
            x = [ordered(r, i, e, m ^ o) for r, o in zip(got, arrays)]
            spots = [me ^ m ^ o for o in arrays]
            if len(x) == 2:
                x = [jnp.where(odd, x[1], x[0]), jnp.where(odd, x[0], x[1])]
                low = (me ^ m) // 2 * 2
                spots = [low, low + 1]
                if part % LANES == 0:
                    x, spots = [jnp.concatenate(x, axis=1)], [low // 2]
            for piece, spot in zip(x, spots):
                size = piece.shape[1]
                at = pl.ds(pl.multiple_of(spot * size, size), size)
                term = jnp.dot(piece, down[e, at, across], preferred_element_type=F32)
                base = term if base is None else base + term
                if cut:
                    continue
                term = lax.dot_general(
                    piece,
                    columns(shrink, spot, size),
                    (((1,), (1,)), ((), ())),
                    preferred_element_type=F32,
                )
                inside = (lane >= e * per) & (lane < (e + 1) * per)
                term = jnp.where(inside, term, 0.0)
                small = term if small is None else small + term
    if opens:
        refs[0][...] = base
        refs[1][...] = small
        rank = per // SLOTS
        away = jnp.full((rows, ranks), -1.0, F32)
        for e in range(experts):
            value = column(meta, lane16, (PIECES + 1) * EXPERTS + first + e)
            for s in range(SLOTS):
                low = e * per + s * rank
                inside = (lane >= low) & (lane < low + rank)
                away = jnp.where(inside, value - (me * SLOTS + s).astype(F32), away)
        refs[2][...] = jnp.where(away == 0.0, 1.0, 0.0)
        for f, m in enumerate(flips):
            for e in range(experts):
                refs[3][f * experts + e] = spread(e, m)
        return
    if cut is None:
        refs[0][...] = base
        refs[1][...] = small
        return
    if cut == 0:
        expand, keep, send, ready = refs
        small = (small * here_ref[...]).astype(BF)
        ready[...] = small
    else:
        expand, ready, keep, send = refs
        small = ready[...]
    size = cols // PARTS
    for c in range(n):
        here = slice(c * size, (c + 1) * size)
        there = slice(c * cols + across.start, c * cols + across.stop)
        out = jnp.dot(small, expand[:, there], preferred_element_type=F32)
        out += jnp.where(me == c, base, 0.0)
        keep[:, here] = out[:half]
        send[:, here] = out[half:].astype(BF)


def add_and_deal(size, count, sets, *refs):
    ins, outs = refs[: count * sets], refs[count * sets :]
    width = ins[0].shape[1]
    for s in range(sets):
        total = ins[s * count][...]
        for r in ins[s * count + 1 : (s + 1) * count]:
            total += r[...].astype(F32)
        parts = [total[r : r + size] for r in range(0, total.shape[0], size)]
        for i, o in enumerate(outs):
            dealt = jnp.concatenate(parts[i :: len(outs)], axis=0)
            o[:, s * width : (s + 1) * width] = dealt.astype(o.dtype)


def finish(cols, *refs):
    total = refs[0][...]
    for r in refs[1:-1]:
        total += r[...].astype(F32)
    size, n = cols // PARTS, total.shape[1] // cols
    for p in range(PARTS):
        for c in range(n):
            at = (p * n + c) * size
            to = c * cols + p * size
            refs[-1][:, to : to + size] = total[:, at : at + size].astype(BF)


def shards(tokens, expert_ids, route_weight, tenant_ids, gate, up, down, shrink, expand, owner, slot):
    n_z, n_dp = lax.axis_size("expert"), lax.axis_size("dp")
    n_x = n_dp // 2
    rows, width = tokens.shape
    experts, _, part = gate.shape
    wide = width + LANES
    block = rows * n_x
    half_rows = block * n_z
    all_rows = 2 * half_rows
    x_bits = [b for b in (2, 4, 8, 16, 32, 64) if b < n_dp]

    def over(x, axis, m):
        return lax.ppermute(x, axis, [(i, i ^ m) for i in range(lax.axis_size(axis))])

    inputs = (tenant_ids, tokens, expert_ids, route_weight, owner, slot)
    weights = [in_hbm(a) for a in (gate, up, down)]
    with jax.named_scope("prepare"):
        y = call(
            prepare,
            shape((rows, wide)),
            [*[in_hbm(a) for a in inputs], *weights],
            [HB] * (len(inputs) + 3),
            scratch=[
                *[(pltpu.VMEM if i else pltpu.SMEM)(a.shape, a.dtype) for i, a in enumerate(inputs)],
                pltpu.SemaphoreType.DMA((len(inputs),)),
            ],
        )

    blocks = [y]
    for b in x_bits:
        blocks = blocks + [over(a, "dp", b) for a in blocks]
    with jax.named_scope("join"):
        lead = call(
            functools.partial(join_blocks, n_x),
            shape((block, wide)),
            (*blocks, *weights),
            [VM] * n_x + [HB] * 3,
            room=(2 << 20) + 4 * block * wide,
        )
    along_z = {k: over(lead, "expert", k) if k else lead for k in range(n_z)}
    places = [0, *range(2, n_z), 1]
    places += [k + n_z for k in places]
    gathered = [along_z[k] for k in places[:n_z]]
    gathered += [over(a, "dp", 1) for a in gathered]

    lists = [list(range(experts))]
    if experts > 1:
        lists = [lists[0][: experts // 2], lists[0][experts // 2 :]]
    packed_rows = all_rows // rows * CAP
    with jax.named_scope("gather"):
        xs, info = call(
            functools.partial(gather_rows, places),
            [shape((all_rows, width)), shape((all_rows, LANES))],
            gathered,
        )
    hidden = []
    for picked in lists:
        with jax.named_scope("up"):
            outs = [shape((len(picked), all_rows, part))]
            if picked is lists[-1]:
                outs.append(shape((len(picked), packed_rows, part)))
            h, *packed = call(
                functools.partial(up_kernel, picked, rows),
                outs,
                (xs, info, in_vmem(gate), in_vmem(up)),
                room=(4 << 20) + 4 * all_rows * (packed_rows + 4 * part + 8 * LANES),
            )
        hidden.append({0: h, "sent": packed[0] if packed else h})
    for got in hidden:
        moved = {0: got["sent"]}
        for b in x_bits:
            moved.update({m | b: over(a, "dp", b) for m, a in moved.items()})
        got.update({m: a for m, a in moved.items() if m})

    def between_cores(got, pairs, behind=()):
        for m in pairs:
            x = got[m] if m else got["sent"]
            if behind:
                x = got[m] = call(relay, shape(x.shape), (x, *behind), in_place=True)
            got[m ^ 1] = over(x, "dp", 1)

    others = list(range(2, n_dp, 2))
    for got in hidden:
        between_cores(got, [0] if got is hidden[-1] else [0, *others])

    shrink2 = shrink.reshape(-1, shrink.shape[-1])
    expand2 = expand.reshape(-1, expand.shape[-1])
    cols = down.shape[2]
    ranks = shrink2.shape[0]
    sums = [shape((all_rows, cols), F32), shape((all_rows, ranks), F32)]
    spreads = shape(((n_dp - 2) * experts, all_rows, packed_rows))
    flips = list(range(2, n_dp)) if size_of(spreads) < 1 << 20 else []
    both, last = (0, 1), len(lists) - 1
    steps = [[(0, i, both) for i in range(len(lists))]]
    steps[0] += [(m, i, (0,)) for i in range(last) for m in others]
    steps += [[(m, i, (int(i < last),)) for i in range(len(lists)) for m in others]]
    steps += [[(m, last, (1,)) for m in others]]
    carried, routing = [], []

    def add_terms(step, opens, cut, outs, after):
        arrays = [hidden[i][m ^ o] for m, i, cores in step for o in cores]
        terms = [(m, lists[i], cores) for m, i, cores in step]
        with jax.named_scope("down"):
            return call(
                functools.partial(down_kernel, rows, n_dp, flips, terms, opens, cut),
                outs,
                [*arrays, *(info, in_vmem(down), shrink2), *carried, *routing, *after],
                room=(6 << 20) + 4 * all_rows * (4 * cols + 2 * packed_rows + 4 * part),
            )

    for s, step in enumerate(steps[:-1]):
        if s == 1:
            between_cores(hidden[-1], others, carried)
        outs = list(sums)
        if s == 0:
            outs += [shape((all_rows, ranks), F32)] + ([spreads] if flips else [])
        carried = add_terms(step, s == 0, None, outs, [])
        if s == 0:
            carried, routing = carried[:2], carried[2:]

    some = width // PARTS
    arrived, after = [], [expand2]
    for cut in range(PARTS):
        outs = [shape((half_rows, some), F32), shape((half_rows, some))]
        ready = shape((all_rows, ranks))
        keep, send, *more = add_terms(
            steps[-1], False, cut, outs + ([ready] if cut == 0 else []), after
        )
        after = after + more
        terms, left = [keep, over(send, "dp", 1)], n_x
        for b in x_bits[::-1]:
            left //= 2
            dims = (n_z * left * rows, some)
            kept = call(
                functools.partial(add_and_deal, left * rows, 2, 1),
                [shape(dims, F32), shape(dims)],
                terms,
                room=(2 << 20) + 3 * size_of(terms[0]),
            )
            terms = [kept[0], over(kept[1], "dp", b)]
        arrived += terms
    kept = call(
        functools.partial(add_and_deal, rows, 2, PARTS),
        [shape((rows, width), F32)] + [shape((rows, width))] * (n_z - 1),
        arrived,
        room=(2 << 20) + 6 * size_of(arrived[0]),
    )
    back = [over(kept[k], "expert", k) for k in [n_z - 1, *range(1, n_z - 1)]]
    with jax.named_scope("finish"):
        return call(
            functools.partial(finish, cols),
            shape((rows, width)),
            [kept[0], *back],
        )


def solution(mesh):
    rows = ("group", "expert", "dp")
    in_specs = (
        P(rows, None),
        P(rows, None),
        P(rows, None),
        P(rows),
        P("expert", None, "dp"),
        P("expert", None, "dp"),
        P("expert", None, "dp"),
        P("expert", "dp", None, None),
        P("expert", "dp", None, None),
        P(),
        P(),
    )
    return jax.shard_map(
        shards, mesh=mesh, in_specs=in_specs, out_specs=P(rows, None), check_vma=False
    )
```
